512 devices in a mesh: space: 32 (over y, z_lo), mode: 16 (over x, z_hi, core).
Axes of the slice: x: 4, y: 8, z: 8 (z_hi: 2, z_lo: 4; z = z_hi * 4 + z_lo), core: 2. Of those that a mesh axis runs over, the one named last changes fastest.
Arguments:
- old_modes: bfloat16 [512, 64, 4096], P('mode', None, 'space'), as said below
- new_modes: bfloat16 [512, 64, 4096], P('mode', None, 'space'), as said below
- material: int32 [64, 4096], P(None, 'space'), may hold values from 0 to 11
- density: float32 [12], replicated, may hold values from 0.5 to 2
- memb_x: bfloat16 [12], replicated, may hold values from 1 to 4
- memb_y: bfloat16 [12], replicated, may hold values from 1 to 4
- bend_table: float32 [12], replicated, may hold values from 0.02 to 0.1
Outputs:
- cross_mass: float32 [512, 512], P(None, 'mode')
- cross_membrane: float32 [512, 512], P(None, 'mode')
- cross_bending: float32 [512, 512], P(None, 'mode')
- mass_image: bfloat16 [512, 64, 4096], P('mode', None, 'space')
- stiff_image: bfloat16 [512, 64, 4096], P('mode', None, 'space')
The draws below stay inside these ranges and needn't reach their ends.
Inputs may be any that keep to these rules, and one draw needn't show every extreme that they name: `old_modes`: A value of one mode shape at one cell. `new_modes`: A value of one mode shape at one cell.
All inputs are finite; a program needn't handle non-finite values.
Results may differ from the reference program's by a relative error of at most 0.0015.
Values may be sent and summed in bfloat16 or wider, within the bound.
No kernel may reach another device: no remote copies, remote signals or barrier semaphores. Data moves between devices by JAX's collectives and lax.ppermute only.
A program may use at most 64 MiB of HBM per device.

```python
import math
import jax
import jax.numpy as jnp
from jax import lax

K = 512
NMAT = 12
NX = 64
NY = 4096


def mode_fields(key):
    first, second = jax.random.split(jax.random.fold_in(key, 7), 2)
    base = jax.random.normal(first, (K, NX, NY), jnp.float32)
    fresh = jax.random.normal(second, (K, NX, NY), jnp.float32)
    older = base
    newer = 0.7 * base + 0.45 * jnp.roll(base, 1, axis=0) + 0.5 * fresh
    return (jnp.clip(older, -6.0, 6.0), jnp.clip(newer, -6.0, 6.0))


def draw_old_modes(key, part):
    return mode_fields(key)[0].astype(jnp.bfloat16)


def draw_new_modes(key, part):
    return mode_fields(key)[1].astype(jnp.bfloat16)


def plant(result, rng, smallest, largest):
    longest = result.shape.index(max(result.shape))
    spots = []
    for shift in (0, 1):
        where = [jax.random.randint(jax.random.fold_in(rng, axis), (), 0, length) for axis, length in enumerate(result.shape)]
        where[longest] = (where[longest] + shift) % result.shape[longest]
        spots.append(tuple(where))
    return result.at[spots[0]].set(smallest).at[spots[1]].set(largest)


def setup_inputs(seed: int = 0) -> dict:
    streams_of = jax.random.split(jax.random.key(seed), 8)
    return {
        "old_modes": draw_old_modes(jax.random.fold_in(streams_of[7], 71), 0),
        "new_modes": draw_new_modes(jax.random.fold_in(streams_of[7], 71), 0),
        "material": plant(jax.random.randint(streams_of[2], (NX, NY), 0, NMAT), jax.random.fold_in(streams_of[2], 1), 0, NMAT - 1).astype(jnp.int32),
        "density": jnp.clip(jnp.exp(jax.random.uniform(streams_of[3], (NMAT,), jnp.float32, math.log(0.5), math.log(2.0))), 0.5, 2.0),
        "memb_x": jnp.clip(jnp.exp(jax.random.uniform(streams_of[4], (NMAT,), jnp.float32, math.log(1.0), math.log(4.0))), 1.0, 4.0).astype(jnp.bfloat16),
        "memb_y": jnp.clip(jnp.exp(jax.random.uniform(streams_of[5], (NMAT,), jnp.float32, math.log(1.0), math.log(4.0))), 1.0, 4.0).astype(jnp.bfloat16),
        "bend_table": jnp.clip(jnp.exp(jax.random.uniform(streams_of[6], (NMAT,), jnp.float32, math.log(0.02), math.log(0.1))), 0.02, 0.1),
    }


def lookup(material, table):
    levels = jnp.arange(table.shape[0], dtype=jnp.int32)
    picks = (material[None, :, :] == levels[:, None, None]).astype(jnp.float32)
    return jnp.sum(picks * table.astype(jnp.float32)[:, None, None], axis=0)


def operators(padded, kxp, kyp, density_field, bend_field, rows, cols):
    def moved(a, b):
        return padded[:, 2 + a:2 + a + rows, 2 + b:2 + b + cols]

    center = moved(0, 0)
    east = moved(1, 0)
    west = moved(-1, 0)
    north = moved(0, 1)
    south = moved(0, -1)
    nearest = east + west + north + south
    mass = density_field * (2.0 / 3.0 * center + nearest / 12.0)
    face_e = 0.5 * (kxp[1:-1, 1:-1] + kxp[2:, 1:-1])
    face_w = 0.5 * (kxp[1:-1, 1:-1] + kxp[:-2, 1:-1])
    face_n = 0.5 * (kyp[1:-1, 1:-1] + kyp[1:-1, 2:])
    face_s = 0.5 * (kyp[1:-1, 1:-1] + kyp[1:-1, :-2])
    membrane = face_e * (center - east) + face_w * (center - west) + face_n * (center - north) + face_s * (center - south)
    diagonals = moved(1, 1) + moved(1, -1) + moved(-1, 1) + moved(-1, -1)
    distant = moved(2, 0) + moved(-2, 0) + moved(0, 2) + moved(0, -2)
    bending = bend_field * (20.0 * center - 8.0 * nearest + 2.0 * diagonals + distant)
    return mass, membrane, bending


def reference(old_modes, new_modes, material, density, memb_x, memb_y, bend_table):
    count, rows, cols = new_modes.shape
    density_field = lookup(material, density)
    kxp = jnp.pad(lookup(material, memb_x), 1)
    kyp = jnp.pad(lookup(material, memb_y), 1)
    bend_field = lookup(material, bend_table)
    width = 32
    area = 1.0 / (rows * cols)
    flat_old = old_modes.reshape(count, rows * cols).astype(jnp.float32)

    def gram(values):
        return lax.dot_general(flat_old, values.reshape(width, rows * cols), (((1,), (1,)), ((), ())),
                               precision=lax.Precision.HIGHEST,
                               preferred_element_type=jnp.float32) * area

    def one_block(block):
        padded = jnp.pad(block.astype(jnp.float32), ((0, 0), (2, 2), (2, 2)))
        mass, membrane, bending = operators(padded, kxp, kyp, density_field, bend_field, rows, cols)
        return (mass.astype(jnp.bfloat16), (membrane + bending).astype(jnp.bfloat16),
                gram(mass), gram(membrane), gram(bending))

    blocks = new_modes.reshape(count // width, width, rows, cols)
    mass_b, stiff_b, gm, gk, gb = lax.map(one_block, blocks)
    mass_image = mass_b.reshape(count, rows, cols)
    stiff_image = stiff_b.reshape(count, rows, cols)

    def columns(parts):
        return jnp.transpose(parts, (1, 0, 2)).reshape(count, count)

    return columns(gm), columns(gk), columns(gb), mass_image, stiff_image
```

```python
import jax
import jax.numpy as jnp
from jax import lax
from jax.experimental import pallas as pl
from jax.experimental.pallas import tpu as pltpu
from jax.sharding import Mesh, PartitionSpec as P

SPACE = ("y", "zl")
MODE = ("x", "zh", "c")
R, M, C = 64, 32, 128
F32, BF16 = jnp.float32, jnp.bfloat16
VM = pl.BlockSpec(memory_space=pltpu.VMEM)
SM = pl.BlockSpec(memory_space=pltpu.SMEM)


def shifted(value, axis, step):
    n = lax.axis_size(axis)
    return lax.ppermute(value, axis, [(i, (i + step) % n) for i in range(n)])


def select_table(material, table_ref):
    value = jnp.zeros(material.shape, F32)
    for level in range(table_ref.shape[0]):
        value = jnp.where(material == level, table_ref[level].astype(F32), value)
    return value


def edges_kernel(u_ref, mat_ref, my_ref, out_ref, ky):
    ky[...] = select_table(mat_ref[...], my_ref)
    lane = lax.broadcasted_iota(jnp.int32, (1, C), 1)

    def row(r, carry):
        first, last, kfirst, klast = carry
        here = lane // 2 == r
        u = u_ref[r].astype(F32)
        k = jnp.broadcast_to(ky[pl.ds(r, 1), :], (8, C))
        first = jnp.where(here, pltpu.roll(u, 2 * r, 1), first)
        last = jnp.where(here, pltpu.roll(u, (2 * r + 2) % C, 1), last)
        kfirst = jnp.where(here, pltpu.roll(k, 2 * r, 1), kfirst)
        klast = jnp.where(here, pltpu.roll(k, (2 * r + 2) % C, 1), klast)
        return first, last, kfirst, klast

    zu, zk = jnp.zeros((M, C), F32), jnp.zeros((8, C), F32)
    first, last, kfirst, klast = lax.fori_loop(0, R, row, (zu, zu, zk, zk))
    out_ref[0] = jnp.concatenate([first, kfirst], axis=0).astype(BF16)
    out_ref[1] = jnp.concatenate([last, klast], axis=0).astype(BF16)


def edges(u, material, memb_y):
    return pl.pallas_call(
        edges_kernel,
        out_shape=jax.ShapeDtypeStruct((2, M + 8, C), BF16),
        in_specs=[VM, VM, SM],
        out_specs=VM,
        scratch_shapes=[pltpu.VMEM((R, C), F32)],
        cost_estimate=pl.CostEstimate(flops=10**6, bytes_accessed=10**6, transcendentals=0),
    )(u, material, memb_y)


def fields_kernel(mat_ref, left_ref, right_ref, rho_ref, mx_ref, my_ref, dd_ref, f_ref, kx, ky, rho, dd):
    material = mat_ref[...]
    kx[...] = jnp.zeros(kx.shape, F32)
    kx[8 : 8 + R, :] = select_table(material, mx_ref)
    ky[...] = select_table(material, my_ref)
    rho[...] = select_table(material, rho_ref)
    dd[...] = select_table(material, dd_ref)
    lane = lax.broadcasted_iota(jnp.int32, (1, C), 1)
    left = left_ref[M : M + 8, :].astype(F32)
    right = right_ref[M : M + 8, :].astype(F32)

    def row(r, _):
        k = ky[pl.ds(r, 1), :]
        kl = pltpu.roll(left, C - 1 - 2 * r, 1)[0:1]
        kr = pltpu.roll(right, C - 1 - 2 * r, 1)[0:1]
        k8 = jnp.broadcast_to(k, (8, C))
        south = jnp.where(lane == 0, kl, pltpu.roll(k8, 1, 1)[0:1])
        north = jnp.where(lane == C - 1, kr, pltpu.roll(k8, C - 1, 1)[0:1])
        kc = kx[pl.ds(r + 8, 1), :]
        fe = 0.5 * (kc + kx[pl.ds(r + 9, 1), :])
        fw = 0.5 * (kc + kx[pl.ds(r + 7, 1), :])
        fn = 0.5 * (k + north)
        fs = 0.5 * (k + south)
        rr = rho[pl.ds(r, 1), :]
        rows = [rr * (2.0 / 3.0), rr * (1.0 / 12.0), fe + fw + fn + fs, fe, fw, fn, fs, dd[pl.ds(r, 1), :]]
        f_ref[r] = jnp.concatenate(rows, axis=0)
        return 0

    lax.fori_loop(0, R, row, 0)


def fields(material, left, right, density, memb_x, memb_y, bend_table):
    return pl.pallas_call(
        fields_kernel,
        out_shape=jax.ShapeDtypeStruct((R, 8, C), F32),
        in_specs=[VM, VM, VM, SM, SM, SM, SM],
        out_specs=VM,
        scratch_shapes=[pltpu.VMEM((R + 16, C), F32)] + [pltpu.VMEM((R, C), F32)] * 3,
        cost_estimate=pl.CostEstimate(flops=10**6, bytes_accessed=10**6, transcendentals=0),
    )(material, left, right, density, memb_x, memb_y, bend_table)


def stencil_kernel(with_images, u_ref, halo_ref, f_ref, *rest):
    if with_images:
        hi_ref, lo_ref, mass_ref, stiff_ref, us, s1, s2, q = rest
    else:
        hi_ref, lo_ref, us, s1, s2, q = rest
    zero = jnp.zeros((M, C), F32)
    for r in (0, 1, R + 2, R + 3):
        us[r] = zero
    s1[0] = zero
    s1[R + 1] = zero
    lane = lax.broadcasted_iota(jnp.int32, (1, C), 1)
    left = halo_ref[0].astype(F32)[0:M]
    right = halo_ref[1].astype(F32)[0:M]

    def spread(r, _):
        u = u_ref[r].astype(F32)
        south = jnp.where(lane == 0, pltpu.roll(left, C - 1 - 2 * r, 1), pltpu.roll(u, 1, 1))
        south2 = jnp.where(lane < 2, pltpu.roll(left, (C - 2 * r) % C, 1), pltpu.roll(u, 2, 1))
        north = jnp.where(lane == C - 1, pltpu.roll(right, C - 1 - 2 * r, 1), pltpu.roll(u, C - 1, 1))
        north2 = jnp.where(lane >= C - 2, pltpu.roll(right, C - 2 - 2 * r, 1), pltpu.roll(u, C - 2, 1))
        us[r + 2] = u
        s1[r + 1] = south + north
        s2[r] = south2 + north2
        q[r] = f_ref[r, 5:6, :] * north + f_ref[r, 6:7, :] * south
        return 0

    lax.fori_loop(0, R, spread, 0, unroll=4)

    def row(r, _):
        u, east, west = us[r + 2], us[r + 3], us[r + 1]
        near = (east + west) + s1[r + 1]
        mass = f_ref[r, 0:1, :] * u + f_ref[r, 1:2, :] * near
        membrane = f_ref[r, 2:3, :] * u - f_ref[r, 3:4, :] * east - f_ref[r, 4:5, :] * west - q[r]
        far = (us[r + 4] + us[r]) + s2[r]
        diagonal = s1[r] + s1[r + 2]
        bending = f_ref[r, 7:8, :] * (20.0 * u - 8.0 * near + 2.0 * diagonal + far)
        for i, v in enumerate((mass, membrane, bending)):
            hi = v.astype(BF16)
            hi_ref[r, M * i : M * i + M, :] = hi
            lo_ref[r, M * i : M * i + M, :] = (v - hi.astype(F32)).astype(BF16)
        if with_images:
            mass_ref[r] = mass.astype(BF16)
            stiff_ref[r] = (membrane + bending).astype(BF16)
        return 0

    lax.fori_loop(0, R, row, 0, unroll=4)


def stencil(u, halo, f, with_images):
    terms = [jax.ShapeDtypeStruct((R, 3 * M, C), BF16)] * 2
    images = [jax.ShapeDtypeStruct((R, M, C), BF16)] * (2 if with_images else 0)
    return pl.pallas_call(
        lambda *refs: stencil_kernel(with_images, *refs),
        out_shape=terms + images,
        in_specs=[VM] * 3,
        out_specs=[VM] * (len(terms) + len(images)),
        scratch_shapes=[
            pltpu.VMEM((R + 4, M, C), F32),
            pltpu.VMEM((R + 2, M, C), F32),
            pltpu.VMEM((R, M, C), F32),
            pltpu.VMEM((R, M, C), F32),
        ],
        compiler_params=pltpu.CompilerParams(vmem_limit_bytes=24 * 2**20),
        cost_estimate=pl.CostEstimate(flops=10**7, bytes_accessed=4 * 10**6, transcendentals=0),
    )(u, halo, f)


STEP = 8


def gram_kernel(*refs):
    terms, olds, out_ref, acc = refs[:8], refs[8:12], refs[12], refs[13]
    step = pl.program_id(0)

    def wide(ref):
        return jnp.concatenate([ref[r] for r in range(STEP)], axis=1)

    old = jnp.concatenate([wide(o) for o in olds], axis=0)

    @pl.when(step == 0)
    def _():
        acc[...] = jnp.zeros(acc.shape, F32)

    dims = (((1,), (1,)), ((), ()))
    for d in range(4):
        part = lax.dot_general(wide(terms[2 * d]), old, dims, preferred_element_type=F32)
        part += lax.dot_general(wide(terms[2 * d + 1]), old, dims, preferred_element_type=F32)
        acc[d] += part

    @pl.when(step == R // STEP - 1)
    def _():
        x, zh, c = lax.axis_index("x"), lax.axis_index("zh"), lax.axis_index("c")
        lane = lax.broadcasted_iota(jnp.int32, (1, 4 * M), 1)
        for d in range(4):
            v = pltpu.roll(acc[d], zh * 64, 1)
            swapped = jnp.where(lane % 64 < 32, pltpu.roll(v, 96, 1), pltpu.roll(v, 32, 1))
            v = jnp.where(c == 1, swapped, v)
            place = lax.rem(x + d, 4)
            for i in range(8):
                out_ref[i, place] = v[12 * i : 12 * i + 12]


def gram(terms, olds):
    return pl.pallas_call(
        gram_kernel,
        grid=(R // STEP,),
        out_shape=jax.ShapeDtypeStruct((8, 4, 12, 4 * M), F32),
        in_specs=[pl.BlockSpec((STEP, 3 * M, C), lambda i: (i, 0, 0))] * 8
        + [pl.BlockSpec((STEP, M, C), lambda i: (i, 0, 0))] * 4,
        out_specs=pl.BlockSpec((8, 4, 12, 4 * M), lambda i: (0, 0, 0, 0)),
        scratch_shapes=[pltpu.VMEM((4, 3 * M, 4 * M), F32)],
        compiler_params=pltpu.CompilerParams(vmem_limit_bytes=24 * 2**20),
        cost_estimate=pl.CostEstimate(flops=2 * 10**9, bytes_accessed=14 * 10**6, transcendentals=0),
    )(*terms, *olds)


def local(old_modes, new_modes, material, density, memb_x, memb_y, bend_table):
    old = old_modes.transpose(1, 0, 2)
    new = new_modes.transpose(1, 0, 2)
    other = shifted(old, "zh", 1)
    packet = edges(new, material, memb_y.astype(F32))
    n = 32
    up = [(i, i + 1) for i in range(n - 1)]
    down = [(i + 1, i) for i in range(n - 1)]
    left = lax.ppermute(packet[1], SPACE, up)
    right = lax.ppermute(packet[0], SPACE, down)
    panels = [new] + [shifted(new, "x", -d) for d in (1, 2, 3)]
    halo = jnp.stack([left, right])
    halos = lax.all_to_all(jnp.broadcast_to(halo[None], (4, *halo.shape)), "x", 0, 0)
    x = lax.axis_index("x")
    old_core = shifted(old, "c", 1)
    other_core = shifted(other, "c", 1)
    f = fields(material, left, right, density, memb_x.astype(F32), memb_y.astype(F32), bend_table)
    hi0, lo0, mass, stiff = stencil(new, halo, f, True)
    terms = [hi0, lo0]
    return finish(terms, panels, halos, x, f, (old, old_core, other, other_core), mass, stiff)


def field_terms(panel, halos, x, d, f):
    return stencil(panel, lax.dynamic_index_in_dim(halos, lax.rem(x + d, 4), 0, keepdims=False), f, False)


def finish(terms, panels, halos, x, f, olds, mass, stiff):
    for d in (1, 2, 3):
        terms = terms + list(field_terms(panels[d], halos, x, d, f))
    part = gram(terms, olds)
    part = jnp.sum(lax.all_to_all(part, "y", 0, 0), axis=0)
    part = jnp.broadcast_to(part[:, None], (4, 4, 12, 4 * M)).reshape(16, 12, 4 * M)
    part = lax.all_to_all(part, ("x", "zl"), 0, 0).reshape(4, 4, 12, 4 * M)
    part = jnp.sum(part, axis=1)
    part = lax.all_to_all(jnp.broadcast_to(part[None], (8, 4, 12, 4 * M)), "y", 0, 0)
    area = 1.0 / (R * C * 32)
    total = part.transpose(0, 2, 1, 3).reshape(3, M, 16 * M) * area
    crosses = [total[i].T for i in range(3)]
    return (*crosses, mass.transpose(1, 0, 2), stiff.transpose(1, 0, 2))


def solution(mesh):
    fine = Mesh(mesh.devices.reshape(8, 4, 4, 2, 2), ("y", "zl", "x", "zh", "c"))
    in_specs = (
        P(MODE, None, SPACE),
        P(MODE, None, SPACE),
        P(None, SPACE),
        P(),
        P(),
        P(),
        P(),
    )
    out_specs = (
        P(None, MODE),
        P(None, MODE),
        P(None, MODE),
        P(MODE, None, SPACE),
        P(MODE, None, SPACE),
    )
    return jax.shard_map(local, mesh=fine, in_specs=in_specs, out_specs=out_specs, check_vma=False)
```

```python
import jax
import jax.numpy as jnp
from jax import lax
from jax.experimental import pallas as pl
from jax.experimental.pallas import tpu as pltpu
from jax.sharding import Mesh, PartitionSpec as P

SPACE = ("y", "zl")
MODE = ("x", "zh", "c")
R, M, C = 64, 32, 128
F32, BF16 = jnp.float32, jnp.bfloat16
VM = pl.BlockSpec(memory_space=pltpu.VMEM)
SM = pl.BlockSpec(memory_space=pltpu.SMEM)


def shifted(value, axis, step):
    n = lax.axis_size(axis)
    return lax.ppermute(value, axis, [(i, (i + step) % n) for i in range(n)])


def select_table(material, tables_ref, which):
    value = jnp.zeros(material.shape, F32)
    for level in range(tables_ref.shape[1]):
        value = jnp.where(material == level, tables_ref[which, level], value)
    return value


def edges_kernel(u_ref, mat_ref, tables_ref, first_ref, last_ref, ky):
    ky[...] = select_table(mat_ref[...], tables_ref, 2)
    pair = lax.broadcasted_iota(jnp.int32, (8, C), 1) // 2
    firsts, lasts = [], []
    for m in range(0, M + 8, 8):
        first = last = jnp.zeros((8, C), F32)
        for r in range(R):
            v = u_ref[r, m : m + 8, :].astype(F32) if m < M else jnp.broadcast_to(ky[r : r + 1, :], (8, C))
            first = jnp.where(pair == r, pltpu.roll(v, 2 * r, 1), first)
            last = jnp.where(pair == r, pltpu.roll(v, (2 * r + 2) % C, 1), last)
        firsts.append(first)
        lasts.append(last)
    first_ref[...] = jnp.concatenate(firsts, axis=0).astype(BF16)
    last_ref[...] = jnp.concatenate(lasts, axis=0).astype(BF16)


def edges(u, material, tables):
    return pl.pallas_call(
        edges_kernel,
        out_shape=[jax.ShapeDtypeStruct((M + 8, C), BF16)] * 2,
        in_specs=[VM, VM, SM],
        out_specs=[VM] * 2,
        scratch_shapes=[pltpu.VMEM((R, C), F32)],
        cost_estimate=pl.CostEstimate(flops=10**6, bytes_accessed=10**6, transcendentals=0),
    )(u, material, tables)


def fields_kernel(mat_ref, left_ref, right_ref, tables_ref, f_ref, kx, ky, rho, dd):
    material = mat_ref[...]
    kx[...] = jnp.zeros(kx.shape, F32)
    kx[8 : 8 + R, :] = select_table(material, tables_ref, 1)
    ky[...] = select_table(material, tables_ref, 2)
    rho[...] = select_table(material, tables_ref, 0)
    dd[...] = select_table(material, tables_ref, 3)
    lane = lax.broadcasted_iota(jnp.int32, (1, C), 1)
    left = left_ref[M : M + 8, :].astype(F32)
    right = right_ref[M : M + 8, :].astype(F32)

    for r in range(R):
        k = ky[r : r + 1, :]
        kl = pltpu.roll(left, C - 1 - 2 * r, 1)[0:1]
        kr = pltpu.roll(right, C - 1 - 2 * r, 1)[0:1]
        k8 = jnp.broadcast_to(k, (8, C))
        south = jnp.where(lane == 0, kl, pltpu.roll(k8, 1, 1)[0:1])
        north = jnp.where(lane == C - 1, kr, pltpu.roll(k8, C - 1, 1)[0:1])
        kc = kx[r + 8 : r + 9, :]
        fe = 0.5 * (kc + kx[r + 9 : r + 10, :])
        fw = 0.5 * (kc + kx[r + 7 : r + 8, :])
        fn = 0.5 * (k + north)
        fs = 0.5 * (k + south)
        rr = rho[r : r + 1, :]
        rows = [rr * (2.0 / 3.0), rr * (1.0 / 12.0), fe + fw + fn + fs, fe, fw, fn, fs, dd[r : r + 1, :]]
        f_ref[r] = jnp.concatenate(rows, axis=0)


def fields(material, left, right, tables):
    return pl.pallas_call(
        fields_kernel,
        out_shape=jax.ShapeDtypeStruct((R, 8, C), F32),
        in_specs=[VM, VM, VM, SM],
        out_specs=VM,
        scratch_shapes=[pltpu.VMEM((R + 16, C), F32)] + [pltpu.VMEM((R, C), F32)] * 3,
        cost_estimate=pl.CostEstimate(flops=10**6, bytes_accessed=10**6, transcendentals=0),
    )(material, left, right, tables)


PIECE = 3 * M // 8
ROWS = 8


def panel_kernel(with_images, appends, u_ref, halo_ref, f_ref, *rest):
    olds, rest = rest[:4], rest[4:]
    before_ref, rest = (rest[0], rest[1:]) if appends else (None, rest)
    if with_images:
        out_ref, mass_ref, stiff_ref, us, s1, s2, q, img, acc = rest
    else:
        out_ref, us, s1, s2, q, img, acc = rest
    zero = jnp.zeros((M, C), F32)
    for r in (0, 1, R + 2, R + 3):
        us[r] = zero
    s1[0] = zero
    s1[R + 1] = zero
    lane = lax.broadcasted_iota(jnp.int32, (1, C), 1)
    left = halo_ref[0].astype(F32)[0:M]
    right = halo_ref[1].astype(F32)[0:M]
    first = jnp.where(lane % 2 == 0, right, left)
    right = pltpu.roll(right, C - 2, 1)
    second = [jnp.where((lane // 2) % 2 == p, left, right) for p in (0, 1)]

    for r in range(R):
        u = u_ref[r].astype(F32)
        h1 = pltpu.roll(first, C - 1 - 2 * r, 1)
        h2 = pltpu.roll(second[r % 2], (C - 2 * r) % C, 1)
        south = jnp.where(lane == 0, h1, pltpu.roll(u, 1, 1))
        south2 = jnp.where(lane < 2, h2, pltpu.roll(u, 2, 1))
        north = jnp.where(lane == C - 1, h1, pltpu.roll(u, C - 1, 1))
        north2 = jnp.where(lane >= C - 2, h2, pltpu.roll(u, C - 2, 1))
        us[r + 2] = u
        s1[r + 1] = south + north
        s2[r] = south2 + north2
        q[r] = f_ref[r, 5:6, :] * north + f_ref[r, 6:7, :] * south

    acc[...] = jnp.zeros(acc.shape, F32)

    def rows(step, _):
        base = step * ROWS
        for j in range(ROWS):
            r = base + j
            u, east, west = us[r + 2], us[r + 3], us[r + 1]
            near = (east + west) + s1[r + 1]
            mass = f_ref[r, 0:1, :] * u + f_ref[r, 1:2, :] * near
            membrane = f_ref[r, 2:3, :] * u - f_ref[r, 3:4, :] * east - f_ref[r, 4:5, :] * west - q[r]
            far = (us[r + 4] + us[r]) + s2[r]
            diagonal = s1[r] + s1[r + 2]
            bending = f_ref[r, 7:8, :] * (20.0 * u - 8.0 * near + 2.0 * diagonal + far)
            for i, v in enumerate((mass, membrane, bending)):
                hi = v.astype(BF16)
                lo = (v - hi.astype(F32)).astype(BF16)
                img[step % 2, M * i : M * i + M, C * j : C * j + C] = hi
                img[step % 2, M * (i + 3) : M * (i + 3) + M, C * j : C * j + C] = lo
            if with_images:
                mass_ref[r] = mass.astype(BF16)
                stiff_ref[r] = (membrane + bending).astype(BF16)
        wide = [jnp.concatenate([o[base + j] for j in range(ROWS)], axis=1) for o in olds]
        acc[...] += lax.dot_general(
            img[step % 2], jnp.concatenate(wide, axis=0), (((1,), (1,)), ((), ())), preferred_element_type=F32
        )
        return 0

    for step in range(R // ROWS):
        rows(step, 0)
    zh, c = lax.axis_index("zh"), lax.axis_index("c")
    v = pltpu.roll(acc[0 : 3 * M] + acc[3 * M : 6 * M], zh * 64, 1)
    lane = lax.broadcasted_iota(jnp.int32, (1, 4 * M), 1)
    swapped = jnp.where(lane % 64 < 32, pltpu.roll(v, 96, 1), pltpu.roll(v, 32, 1))
    v = jnp.where(c == 1, swapped, v)
    for i in range(8):
        if appends:
            out_ref[i, 0:PIECE] = before_ref[i]
            out_ref[i, PIECE : 2 * PIECE] = v[PIECE * i : PIECE * i + PIECE]
        else:
            out_ref[i] = v[PIECE * i : PIECE * i + PIECE]


def panel(u, halo, f, olds, before, with_images):
    outs = [jax.ShapeDtypeStruct((8, PIECE if before is None else 2 * PIECE, 4 * M), F32)]
    outs += [jax.ShapeDtypeStruct((R, M, C), BF16)] * (2 if with_images else 0)
    operands = [u, halo, f, *olds] + ([] if before is None else [before])
    return pl.pallas_call(
        lambda *refs: panel_kernel(with_images, before is not None, *refs),
        out_shape=outs,
        in_specs=[VM] * len(operands),
        out_specs=[VM] * len(outs),
        scratch_shapes=[
            pltpu.VMEM((R + 4, M, C), F32),
            pltpu.VMEM((R + 2, M, C), F32),
            pltpu.VMEM((R, M, C), F32),
            pltpu.VMEM((R, M, C), F32),
            pltpu.VMEM((2, 6 * M, ROWS * C), BF16),
            pltpu.VMEM((6 * M, 4 * M), F32),
        ],
        compiler_params=pltpu.CompilerParams(vmem_limit_bytes=16 * 2**20),
        cost_estimate=pl.CostEstimate(flops=4 * 10**8, bytes_accessed=4 * 10**6, transcendentals=0),
    )(*operands)


def small(kernel, out_shape, *operands):
    return pl.pallas_call(
        kernel,
        out_shape=out_shape,
        in_specs=[VM] * len(operands),
        out_specs=jax.tree.map(lambda _: VM, out_shape),
        cost_estimate=pl.CostEstimate(flops=10**5, bytes_accessed=4 * 10**5, transcendentals=0),
    )(*operands)


def added(ref, axis_size, *at):
    total = ref[(0, *at)]
    for i in range(1, axis_size):
        total = total + ref[(i, *at)]
    return total


def to_chips_kernel(first_ref, second_ref, out_ref):
    x = lax.axis_index("x")
    first, second = added(first_ref, 8), added(second_ref, 8)
    for d, v in ((0, first[:PIECE]), (1, first[PIECE:]), (3, second[:PIECE]), (2, second[PIECE:])):
        place = lax.rem(x + d, 4) * 4
        for z in range(4):
            out_ref[place + z] = v


def to_y_kernel(in_ref, out_ref):
    for x in range(4):
        v = in_ref[4 * x] + in_ref[4 * x + 1] + in_ref[4 * x + 2] + in_ref[4 * x + 3]
        for y in range(8):
            out_ref[y, PIECE * x : PIECE * x + PIECE] = v


def crosses_kernel(in_ref, mass_ref, membrane_ref, bending_ref):
    area = 1.0 / (R * C * 32)
    for x in range(4):
        v = jnp.concatenate([in_ref[y, PIECE * x : PIECE * x + PIECE] for y in range(8)], axis=0) * area
        for i, ref in enumerate((mass_ref, membrane_ref, bending_ref)):
            ref[:, 4 * M * x : 4 * M * x + 4 * M] = v[M * i : M * i + M]


def local(old_modes, new_modes, material, density, memb_x, memb_y, bend_table):
    tables = jnp.stack([density, memb_x.astype(F32), memb_y.astype(F32), bend_table])
    old = old_modes.transpose(1, 0, 2)
    new = new_modes.transpose(1, 0, 2)
    other = shifted(old, "zh", 1)
    panels = [new] + [shifted(new, "x", -d) for d in (1, 2, 3)]
    first, last = edges(new, material, tables)
    n = 32
    left = lax.ppermute(last, SPACE, [(i, i + 1) for i in range(n - 1)])
    right = lax.ppermute(first, SPACE, [(i + 1, i) for i in range(n - 1)])
    halo = jnp.stack([left, right])
    halos = lax.all_to_all(jnp.broadcast_to(halo[None], (4, *halo.shape)), "x", 0, 0)
    x = lax.axis_index("x")
    beside = [halo] + [lax.dynamic_index_in_dim(halos, lax.rem(x + d, 4), 0, keepdims=False) for d in (1, 2, 3)]
    olds = (old, shifted(old, "c", 1), other, shifted(other, "c", 1))
    f = fields(material, left, right, tables)
    part, mass, stiff = panel(new, halo, f, olds, None, True)
    (part,) = panel(panels[1], beside[1], f, olds, part, False)
    early = lax.all_to_all(part, "y", 0, 0)
    (part,) = panel(panels[3], beside[3], f, olds, None, False)
    (part,) = panel(panels[2], beside[2], f, olds, part, False)
    late = lax.all_to_all(part, "y", 0, 0)
    part = small(to_chips_kernel, jax.ShapeDtypeStruct((16, PIECE, 4 * M), F32), early, late)
    part = lax.all_to_all(part, ("x", "zl"), 0, 0)
    part = small(to_y_kernel, jax.ShapeDtypeStruct((8, 4 * PIECE, 4 * M), F32), part)
    part = lax.all_to_all(part, "y", 0, 0)
    crosses = small(crosses_kernel, [jax.ShapeDtypeStruct((M, 16 * M), F32)] * 3, part)
    return (*[v.T for v in crosses], mass.transpose(1, 0, 2), stiff.transpose(1, 0, 2))


def solution(mesh):
    fine = Mesh(mesh.devices.reshape(8, 4, 4, 2, 2), ("y", "zl", "x", "zh", "c"))
    in_specs = (
        P(MODE, None, SPACE),
        P(MODE, None, SPACE),
        P(None, SPACE),
        P(),
        P(),
        P(),
        P(),
    )
    out_specs = (
        P(None, MODE),
        P(None, MODE),
        P(None, MODE),
        P(MODE, None, SPACE),
        P(MODE, None, SPACE),
    )
    return jax.shard_map(local, mesh=fine, in_specs=in_specs, out_specs=out_specs, check_vma=False)
```

```python
import jax
import jax.numpy as jnp
from jax import lax
from jax.experimental import pallas as pl
from jax.experimental.pallas import tpu as pltpu
from jax.sharding import Mesh, PartitionSpec as P

SPACE = ("y", "zl")
MODE = ("x", "zh", "c")
R, M, C = 64, 32, 128
F32, BF16 = jnp.float32, jnp.bfloat16
VM = pl.BlockSpec(memory_space=pltpu.VMEM)
SM = pl.BlockSpec(memory_space=pltpu.SMEM)


def shifted(value, axis, step):
    n = lax.axis_size(axis)
    return lax.ppermute(value, axis, [(i, (i + step) % n) for i in range(n)])


def select_table(material, tables_ref, which):
    value = jnp.zeros(material.shape, F32)
    for level in range(tables_ref.shape[1]):
        value = jnp.where(material == level, tables_ref[which, level], value)
    return value


def edges_kernel(u_ref, mat_ref, tables_ref, first_ref, last_ref, ky):
    ky[...] = select_table(mat_ref[...], tables_ref, 2)
    pair = lax.broadcasted_iota(jnp.int32, (8, C), 1) // 2
    firsts, lasts = [], []
    for m in range(0, M + 8, 8):
        first = last = jnp.zeros((8, C), F32)
        for r in range(R):
            v = u_ref[r, m : m + 8, :].astype(F32) if m < M else jnp.broadcast_to(ky[r : r + 1, :], (8, C))
            first = jnp.where(pair == r, pltpu.roll(v, 2 * r, 1), first)
            last = jnp.where(pair == r, pltpu.roll(v, (2 * r + 2) % C, 1), last)
        firsts.append(first)
        lasts.append(last)
    first_ref[...] = jnp.concatenate(firsts, axis=0).astype(BF16)
    last_ref[...] = jnp.concatenate(lasts, axis=0).astype(BF16)


def edges(u, material, tables):
    return pl.pallas_call(
        edges_kernel,
        out_shape=[jax.ShapeDtypeStruct((M + 8, C), BF16)] * 2,
        in_specs=[VM, VM, SM],
        out_specs=[VM] * 2,
        scratch_shapes=[pltpu.VMEM((R, C), F32)],
        cost_estimate=pl.CostEstimate(flops=10**6, bytes_accessed=10**6, transcendentals=0),
    )(u, material, tables)


def fields_kernel(mat_ref, left_ref, right_ref, tables_ref, f_ref, kx, ky, rho, dd):
    material = mat_ref[...]
    kx[...] = jnp.zeros(kx.shape, F32)
    kx[8 : 8 + R, :] = select_table(material, tables_ref, 1)
    ky[...] = select_table(material, tables_ref, 2)
    rho[...] = select_table(material, tables_ref, 0)
    dd[...] = select_table(material, tables_ref, 3)
    lane = lax.broadcasted_iota(jnp.int32, (1, C), 1)
    left = left_ref[M : M + 8, :].astype(F32)
    right = right_ref[M : M + 8, :].astype(F32)

    for r in range(R):
        k = ky[r : r + 1, :]
        kl = pltpu.roll(left, C - 1 - 2 * r, 1)[0:1]
        kr = pltpu.roll(right, C - 1 - 2 * r, 1)[0:1]
        k8 = jnp.broadcast_to(k, (8, C))
        south = jnp.where(lane == 0, kl, pltpu.roll(k8, 1, 1)[0:1])
        north = jnp.where(lane == C - 1, kr, pltpu.roll(k8, C - 1, 1)[0:1])
        kc = kx[r + 8 : r + 9, :]
        fe = 0.5 * (kc + kx[r + 9 : r + 10, :])
        fw = 0.5 * (kc + kx[r + 7 : r + 8, :])
        fn = 0.5 * (k + north)
        fs = 0.5 * (k + south)
        rr = rho[r : r + 1, :]
        rows = [rr * (2.0 / 3.0), rr * (1.0 / 12.0), fe + fw + fn + fs, fe, fw, fn, fs, dd[r : r + 1, :]]
        f_ref[r] = jnp.concatenate(rows, axis=0)


def fields(material, left, right, tables):
    return pl.pallas_call(
        fields_kernel,
        out_shape=jax.ShapeDtypeStruct((R, 8, C), F32),
        in_specs=[VM, VM, VM, SM],
        out_specs=VM,
        scratch_shapes=[pltpu.VMEM((R + 16, C), F32)] + [pltpu.VMEM((R, C), F32)] * 3,
        cost_estimate=pl.CostEstimate(flops=10**6, bytes_accessed=10**6, transcendentals=0),
    )(material, left, right, tables)


PIECE = 3 * M // 8
ROWS = 8


def panel_kernel(d, u_ref, halo_ref, f_ref, *rest):
    with_images = d == 0
    olds, rest = rest[:4], rest[4 if d == 0 else 5 :]
    if with_images:
        out_ref, mass_ref, stiff_ref, us, s1, s2, q, img, acc = rest
    else:
        out_ref, us, s1, s2, q, img, acc = rest
    zero = jnp.zeros((M, C), F32)
    for r in (0, 1, R + 2, R + 3):
        us[r] = zero
    s1[0] = zero
    s1[R + 1] = zero
    lane = lax.broadcasted_iota(jnp.int32, (1, C), 1)
    left = halo_ref[0].astype(F32)[0:M]
    right = halo_ref[1].astype(F32)[0:M]
    first = jnp.where(lane % 2 == 0, right, left)
    right = pltpu.roll(right, C - 2, 1)
    second = [jnp.where((lane // 2) % 2 == p, left, right) for p in (0, 1)]

    for r in range(R):
        u = u_ref[r].astype(F32)
        h1 = pltpu.roll(first, C - 1 - 2 * r, 1)
        h2 = pltpu.roll(second[r % 2], (C - 2 * r) % C, 1)
        south = jnp.where(lane == 0, h1, pltpu.roll(u, 1, 1))
        south2 = jnp.where(lane < 2, h2, pltpu.roll(u, 2, 1))
        north = jnp.where(lane == C - 1, h1, pltpu.roll(u, C - 1, 1))
        north2 = jnp.where(lane >= C - 2, h2, pltpu.roll(u, C - 2, 1))
        us[r + 2] = u
        s1[r + 1] = south + north
        s2[r] = south2 + north2
        q[r] = f_ref[r, 5:6, :] * north + f_ref[r, 6:7, :] * south

    acc[...] = jnp.zeros(acc.shape, F32)

    def rows(step, _):
        base = step * ROWS
        for j in range(ROWS):
            r = base + j
            u, east, west = us[r + 2], us[r + 3], us[r + 1]
            near = (east + west) + s1[r + 1]
            mass = f_ref[r, 0:1, :] * u + f_ref[r, 1:2, :] * near
            membrane = f_ref[r, 2:3, :] * u - f_ref[r, 3:4, :] * east - f_ref[r, 4:5, :] * west - q[r]
            far = (us[r + 4] + us[r]) + s2[r]
            diagonal = s1[r] + s1[r + 2]
            bending = f_ref[r, 7:8, :] * (20.0 * u - 8.0 * near + 2.0 * diagonal + far)
            for i, v in enumerate((mass, membrane, bending)):
                hi = v.astype(BF16)
                lo = (v - hi.astype(F32)).astype(BF16)
                img[step % 2, M * i : M * i + M, C * j : C * j + C] = hi
                img[step % 2, M * (i + 3) : M * (i + 3) + M, C * j : C * j + C] = lo
            if with_images:
                mass_ref[r] = mass.astype(BF16)
                stiff_ref[r] = (membrane + bending).astype(BF16)
        wide = [jnp.concatenate([o[base + j] for j in range(ROWS)], axis=1) for o in olds]
        acc[...] += lax.dot_general(
            img[step % 2], jnp.concatenate(wide, axis=0), (((1,), (1,)), ((), ())), preferred_element_type=F32
        )
        return 0

    for step in range(R // ROWS):
        rows(step, 0)
    zh, c = lax.axis_index("zh"), lax.axis_index("c")
    v = pltpu.roll(acc[0 : 3 * M] + acc[3 * M : 6 * M], zh * 64, 1)
    lane = lax.broadcasted_iota(jnp.int32, (1, 4 * M), 1)
    swapped = jnp.where(lane % 64 < 32, pltpu.roll(v, 96, 1), pltpu.roll(v, 32, 1))
    v = jnp.where(c == 1, swapped, v)
    chip = lax.rem(lax.axis_index("x") + d, 4)
    for k in range(4):

        @pl.when(chip == k)
        def _():
            for i in range(8):
                out_ref[i, PIECE * k : PIECE * k + PIECE] = v[PIECE * i : PIECE * i + PIECE]


def panel(d, u, halo, f, olds, parts):
    outs = [jax.ShapeDtypeStruct((8, 4 * PIECE, 4 * M), F32)]
    outs += [jax.ShapeDtypeStruct((R, M, C), BF16)] * (2 if d == 0 else 0)
    operands = [u, halo, f, *olds] + ([] if d == 0 else [parts])
    return pl.pallas_call(
        lambda *refs: panel_kernel(d, *refs),
        out_shape=outs,
        in_specs=[VM] * 7 + ([] if d == 0 else [pl.BlockSpec(memory_space=pl.ANY)]),
        out_specs=[VM] * len(outs),
        input_output_aliases={} if d == 0 else {7: 0},
        scratch_shapes=[
            pltpu.VMEM((R + 4, M, C), F32),
            pltpu.VMEM((R + 2, M, C), F32),
            pltpu.VMEM((R, M, C), F32),
            pltpu.VMEM((R, M, C), F32),
            pltpu.VMEM((2, 6 * M, ROWS * C), BF16),
            pltpu.VMEM((6 * M, 4 * M), F32),
        ],
        compiler_params=pltpu.CompilerParams(vmem_limit_bytes=16 * 2**20),
        cost_estimate=pl.CostEstimate(flops=4 * 10**8, bytes_accessed=4 * 10**6, transcendentals=0),
    )(*operands)


def local(old_modes, new_modes, material, density, memb_x, memb_y, bend_table):
    tables = jnp.stack([density, memb_x.astype(F32), memb_y.astype(F32), bend_table])
    old = old_modes.transpose(1, 0, 2)
    new = new_modes.transpose(1, 0, 2)
    other = shifted(old, "zh", 1)
    panels = [new] + [shifted(new, "x", -d) for d in (1, 2, 3)]
    first, last = edges(new, material, tables)
    n = 32
    left = lax.ppermute(last, SPACE, [(i, i + 1) for i in range(n - 1)])
    right = lax.ppermute(first, SPACE, [(i + 1, i) for i in range(n - 1)])
    halo = jnp.stack([left, right])
    halos = lax.all_to_all(jnp.broadcast_to(halo[None], (4, *halo.shape)), "x", 0, 0)
    x = lax.axis_index("x")
    beside = [halo] + [lax.dynamic_index_in_dim(halos, lax.rem(x + d, 4), 0, keepdims=False) for d in (1, 2, 3)]
    other, left, right, beside[1:], panels[1], panels[3] = lax.optimization_barrier(
        (other, left, right, beside[1:], panels[1], panels[3])
    )
    f = fields(material, left, right, tables)
    f, panels[2] = lax.optimization_barrier((f, panels[2]))
    olds = (old, shifted(old, "c", 1), other, shifted(other, "c", 1))
    parts, mass, stiff = panel(0, new, halo, f, olds, None)
    for d in (1, 3, 2):
        (parts,) = panel(d, panels[d], beside[d], f, olds, parts)
    parts = jnp.sum(lax.all_to_all(parts, "y", 0, 0), axis=0).reshape(4, 1, PIECE, 4 * M)
    parts = jnp.broadcast_to(parts, (4, 4, PIECE, 4 * M)).reshape(16, PIECE, 4 * M)
    parts = lax.all_to_all(parts, ("x", "zl"), 0, 0).reshape(4, 4, PIECE, 4 * M)
    parts = jnp.sum(parts, axis=1).reshape(1, 4 * PIECE, 4 * M)
    parts = lax.all_to_all(jnp.broadcast_to(parts, (8, 4 * PIECE, 4 * M)), "y", 0, 0)
    area = 1.0 / (R * C * n)
    total = parts.reshape(8, 4, PIECE, 4 * M).transpose(0, 2, 1, 3).reshape(3, M, 16 * M) * area
    return (*[total[i].T for i in range(3)], mass.transpose(1, 0, 2), stiff.transpose(1, 0, 2))


def solution(mesh):
    fine = Mesh(mesh.devices.reshape(8, 4, 4, 2, 2), ("y", "zl", "x", "zh", "c"))
    in_specs = (
        P(MODE, None, SPACE),
        P(MODE, None, SPACE),
        P(None, SPACE),
        P(),
        P(),
        P(),
        P(),
    )
    out_specs = (
        P(None, MODE),
        P(None, MODE),
        P(None, MODE),
        P(MODE, None, SPACE),
        P(MODE, None, SPACE),
    )
    return jax.shard_map(local, mesh=fine, in_specs=in_specs, out_specs=out_specs, check_vma=False)
```

```python
import jax
import jax.numpy as jnp
from jax import lax
from jax.experimental import pallas as pl
from jax.experimental.pallas import tpu as pltpu
from jax.sharding import Mesh, PartitionSpec as P

SPACE = ("y", "zl")
MODE = ("x", "zh", "c")
R, M, C = 64, 32, 128
F32, BF16 = jnp.float32, jnp.bfloat16
VM = pl.BlockSpec(memory_space=pltpu.VMEM)
SM = pl.BlockSpec(memory_space=pltpu.SMEM)


def shifted(value, axis, step):
    n = lax.axis_size(axis)
    return lax.ppermute(value, axis, [(i, (i + step) % n) for i in range(n)])


def select_table(material, tables_ref, which):
    value = jnp.zeros(material.shape, F32)
    for level in range(tables_ref.shape[1]):
        value = jnp.where(material == level, tables_ref[which, level], value)
    return value


def edges_kernel(u_ref, mat_ref, first_ref, last_ref, mat):
    mat[...] = mat_ref[...].astype(F32)
    pair = lax.broadcasted_iota(jnp.int32, (8, C), 1) // 2
    firsts, lasts = [], []
    for m in range(0, M + 8, 8):
        first = last = jnp.zeros((8, C), F32)
        for r in range(R):
            v = u_ref[r, m : m + 8, :].astype(F32) if m < M else jnp.broadcast_to(mat[r : r + 1, :], (8, C))
            first = jnp.where(pair == r, pltpu.roll(v, 2 * r, 1), first)
            last = jnp.where(pair == r, pltpu.roll(v, (2 * r + 2) % C, 1), last)
        firsts.append(first)
        lasts.append(last)
    first_ref[...] = jnp.concatenate(firsts, axis=0).astype(BF16)
    last_ref[...] = jnp.concatenate(lasts, axis=0).astype(BF16)


def edges(u, material):
    return pl.pallas_call(
        edges_kernel,
        out_shape=[jax.ShapeDtypeStruct((M + 8, C), BF16)] * 2,
        in_specs=[VM, VM],
        out_specs=[VM] * 2,
        scratch_shapes=[pltpu.VMEM((R, C), F32)],
        cost_estimate=pl.CostEstimate(flops=10**6, bytes_accessed=10**6, transcendentals=0),
    )(u, material)


def fields_kernel(mat_ref, left_ref, right_ref, tables_ref, f_ref, kx, ky, rho, dd):
    material = mat_ref[...]
    kx[...] = jnp.zeros(kx.shape, F32)
    kx[8 : 8 + R, :] = select_table(material, tables_ref, 1)
    ky[...] = select_table(material, tables_ref, 2)
    rho[...] = select_table(material, tables_ref, 0)
    dd[...] = select_table(material, tables_ref, 3)
    lane = lax.broadcasted_iota(jnp.int32, (1, C), 1)
    space = lax.axis_index("y") * 4 + lax.axis_index("zl")
    left = select_table(left_ref[M : M + 8, :].astype(F32), tables_ref, 2)
    left = jnp.where(space > 0, left, 0.0)
    right = select_table(right_ref[M : M + 8, :].astype(F32), tables_ref, 2)
    right = jnp.where(space < 31, right, 0.0)

    for r in range(R):
        k = ky[r : r + 1, :]
        kl = pltpu.roll(left, C - 1 - 2 * r, 1)[0:1]
        kr = pltpu.roll(right, C - 1 - 2 * r, 1)[0:1]
        k8 = jnp.broadcast_to(k, (8, C))
        south = jnp.where(lane == 0, kl, pltpu.roll(k8, 1, 1)[0:1])
        north = jnp.where(lane == C - 1, kr, pltpu.roll(k8, C - 1, 1)[0:1])
        kc = kx[r + 8 : r + 9, :]
        fe = 0.5 * (kc + kx[r + 9 : r + 10, :])
        fw = 0.5 * (kc + kx[r + 7 : r + 8, :])
        fn = 0.5 * (k + north)
        fs = 0.5 * (k + south)
        rr = rho[r : r + 1, :]
        rows = [rr * (2.0 / 3.0), rr * (1.0 / 12.0), fe + fw + fn + fs, fe, fw, fn, fs, dd[r : r + 1, :]]
        f_ref[r] = jnp.concatenate(rows, axis=0)


def fields(material, left, right, tables):
    return pl.pallas_call(
        fields_kernel,
        out_shape=jax.ShapeDtypeStruct((R, 8, C), F32),
        in_specs=[VM, VM, VM, SM],
        out_specs=VM,
        scratch_shapes=[pltpu.VMEM((R + 16, C), F32)] + [pltpu.VMEM((R, C), F32)] * 3,
        cost_estimate=pl.CostEstimate(flops=10**6, bytes_accessed=10**6, transcendentals=0),
    )(material, left, right, tables)


PIECE = 3 * M // 8
PANEL_FLOPS = 3 * 10**9
ROWS = 8


def panel_kernel(with_images, u_ref, halo_ref, f_ref, *rest):
    olds, rest = rest[:2], rest[2:]
    if with_images:
        half_ref, img, mass_ref, stiff_ref, us, s1, s2, q, acc = rest
    else:
        half_ref, img, us, s1, s2, q, acc = rest
    zero = jnp.zeros((M, C), F32)
    for r in (0, 1, R + 2, R + 3):
        us[r] = zero
    s1[0] = zero
    s1[R + 1] = zero
    lane = lax.broadcasted_iota(jnp.int32, (1, C), 1)
    left = halo_ref[0].astype(F32)[0:M]
    right = halo_ref[1].astype(F32)[0:M]
    first = jnp.where(lane % 2 == 0, right, left)
    right = pltpu.roll(right, C - 2, 1)
    second = [jnp.where((lane // 2) % 2 == p, left, right) for p in (0, 1)]

    for r in range(R):
        u = u_ref[r].astype(F32)
        h1 = pltpu.roll(first, C - 1 - 2 * r, 1)
        h2 = pltpu.roll(second[r % 2], (C - 2 * r) % C, 1)
        south = jnp.where(lane == 0, h1, pltpu.roll(u, 1, 1))
        south2 = jnp.where(lane < 2, h2, pltpu.roll(u, 2, 1))
        north = jnp.where(lane == C - 1, h1, pltpu.roll(u, C - 1, 1))
        north2 = jnp.where(lane >= C - 2, h2, pltpu.roll(u, C - 2, 1))
        us[r + 2] = u
        s1[r + 1] = south + north
        s2[r] = south2 + north2
        q[r] = f_ref[r, 5:6, :] * north + f_ref[r, 6:7, :] * south

    acc[...] = jnp.zeros(acc.shape, F32)

    def rows(step, _):
        base = step * ROWS
        for j in range(ROWS):
            r = base + j
            u, east, west = us[r + 2], us[r + 3], us[r + 1]
            near = (east + west) + s1[r + 1]
            mass = f_ref[r, 0:1, :] * u + f_ref[r, 1:2, :] * near
            membrane = f_ref[r, 2:3, :] * u - f_ref[r, 3:4, :] * east - f_ref[r, 4:5, :] * west - q[r]
            far = (us[r + 4] + us[r]) + s2[r]
            diagonal = s1[r] + s1[r + 2]
            bending = f_ref[r, 7:8, :] * (20.0 * u - 8.0 * near + 2.0 * diagonal + far)
            for i, v in enumerate((mass, membrane, bending)):
                hi = v.astype(BF16)
                lo = (v - hi.astype(F32)).astype(BF16)
                img[step, M * i : M * i + M, C * j : C * j + C] = hi
                img[step, M * (i + 3) : M * (i + 3) + M, C * j : C * j + C] = lo
            if with_images:
                mass_ref[r] = mass.astype(BF16)
                stiff_ref[r] = (membrane + bending).astype(BF16)
        wide = [jnp.concatenate([o[base + j] for j in range(ROWS)], axis=1) for o in olds]
        acc[...] += lax.dot_general(
            img[step], jnp.concatenate(wide, axis=0), (((1,), (1,)), ((), ())), preferred_element_type=F32
        )
        return 0

    for step in range(R // ROWS):
        rows(step, 0)
    half_ref[...] = acc[0 : 3 * M] + acc[3 * M : 6 * M]


def panel(u, halo, f, olds, with_images):
    outs = [
        jax.ShapeDtypeStruct((3 * M, 2 * M), F32),
        jax.ShapeDtypeStruct((R // ROWS, 6 * M, ROWS * C), BF16),
    ]
    outs += [jax.ShapeDtypeStruct((R, M, C), BF16)] * (2 if with_images else 0)
    return pl.pallas_call(
        lambda *refs: panel_kernel(with_images, *refs),
        out_shape=outs,
        in_specs=[VM] * 5,
        out_specs=[VM] * len(outs),
        scratch_shapes=[
            pltpu.VMEM((R + 4, M, C), F32),
            pltpu.VMEM((R + 2, M, C), F32),
            pltpu.VMEM((R, M, C), F32),
            pltpu.VMEM((R, M, C), F32),
            pltpu.VMEM((6 * M, 2 * M), F32),
        ],
        compiler_params=pltpu.CompilerParams(vmem_limit_bytes=20 * 2**20),
        cost_estimate=pl.CostEstimate(flops=PANEL_FLOPS, bytes_accessed=4 * 10**6, transcendentals=0),
    )(u, halo, f, *olds)


def rest_kernel(*refs):
    halves, terms, olds, out_ref, acc = refs[:4], refs[4:8], refs[8:10], refs[10], refs[11]
    for step in range(R // ROWS):
        base = step * ROWS
        wide = [jnp.concatenate([o[base + j] for j in range(ROWS)], axis=1) for o in olds]
        wide = jnp.concatenate(wide, axis=0)
        for d in range(4):
            part = lax.dot_general(terms[d][step], wide, (((1,), (1,)), ((), ())), preferred_element_type=F32)
            acc[d] = part if step == 0 else acc[d] + part
    x, zh, c = lax.axis_index("x"), lax.axis_index("zh"), lax.axis_index("c")
    lane = lax.broadcasted_iota(jnp.int32, (1, 4 * M), 1)
    for d in range(4):
        v = jnp.concatenate([halves[d][...], acc[d, 0 : 3 * M] + acc[d, 3 * M : 6 * M]], axis=1)
        v = pltpu.roll(v, zh * 64, 1)
        swapped = jnp.where(lane % 64 < 32, pltpu.roll(v, 96, 1), pltpu.roll(v, 32, 1))
        v = jnp.where(c == 1, swapped, v)
        chip = lax.rem(x + d, 4)
        for k in range(4):

            @pl.when(chip == k)
            def _():
                for i in range(8):
                    out_ref[i, PIECE * k : PIECE * k + PIECE] = v[PIECE * i : PIECE * i + PIECE]


def rest(halves, terms, olds):
    operands = (*halves, *terms, *olds)
    return pl.pallas_call(
        rest_kernel,
        out_shape=jax.ShapeDtypeStruct((8, 4 * PIECE, 4 * M), F32),
        in_specs=[VM] * len(operands),
        out_specs=VM,
        scratch_shapes=[pltpu.VMEM((4, 6 * M, 2 * M), F32)],
        compiler_params=pltpu.CompilerParams(vmem_limit_bytes=20 * 2**20),
        cost_estimate=pl.CostEstimate(flops=3 * 10**9, bytes_accessed=14 * 10**6, transcendentals=0),
    )(*operands)


def local(old_modes, new_modes, material, density, memb_x, memb_y, bend_table):
    tables = jnp.stack([density, memb_x.astype(F32), memb_y.astype(F32), bend_table])
    old = old_modes.transpose(1, 0, 2)
    new = new_modes.transpose(1, 0, 2)
    other = shifted(old, "zh", 1)
    first, last = edges(new, material)
    first, last, new = lax.optimization_barrier((first, last, new))
    panels = [new] + [shifted(new, "x", -d) for d in (1, 2, 3)]
    n = 32
    left = lax.ppermute(last, SPACE, [(i, i + 1) for i in range(n - 1)])
    right = lax.ppermute(first, SPACE, [(i + 1, i) for i in range(n - 1)])
    halo = jnp.stack([left, right])
    halos = lax.all_to_all(jnp.broadcast_to(halo[None], (4, *halo.shape)), "x", 0, 0)
    x = lax.axis_index("x")
    f = fields(material, left, right, tables)
    olds = (old, shifted(old, "c", 1))
    halves, terms = [None] * 4, [None] * 4
    halves[0], terms[0], mass, stiff = panel(new, halo, f, olds, True)
    halves[0], other = lax.optimization_barrier((halves[0], other))
    other_core = shifted(other, "c", 1)
    halves[0], other, panels[1], panels[3] = lax.optimization_barrier((halves[0], other, panels[1], panels[3]))
    for d in (1, 3, 2):
        beside = lax.dynamic_index_in_dim(halos, lax.rem(x + d, 4), 0, keepdims=False)
        if d == 2:
            halves[1], panels[2] = lax.optimization_barrier((halves[1], panels[2]))
        halves[d], terms[d] = panel(panels[d], beside, f, olds, False)
    parts = rest(halves, terms, (other, other_core))
    parts = jnp.sum(lax.all_to_all(parts, "y", 0, 0), axis=0).reshape(4, 1, PIECE, 4 * M)
    parts = jnp.broadcast_to(parts, (4, 4, PIECE, 4 * M)).reshape(16, PIECE, 4 * M)
    parts = lax.all_to_all(parts, ("x", "zl"), 0, 0).reshape(4, 4, PIECE, 4 * M)
    parts = jnp.sum(parts, axis=1).reshape(1, 4 * PIECE, 4 * M)
    parts = lax.all_to_all(jnp.broadcast_to(parts, (8, 4 * PIECE, 4 * M)), "y", 0, 0)
    area = 1.0 / (R * C * n)
    total = parts.reshape(8, 4, PIECE, 4 * M).transpose(0, 2, 1, 3).reshape(3, M, 16 * M) * area
    return (*[total[i].T for i in range(3)], mass.transpose(1, 0, 2), stiff.transpose(1, 0, 2))


def solution(mesh):
    fine = Mesh(mesh.devices.reshape(8, 4, 4, 2, 2), ("y", "zl", "x", "zh", "c"))
    in_specs = (
        P(MODE, None, SPACE),
        P(MODE, None, SPACE),
        P(None, SPACE),
        P(),
        P(),
        P(),
        P(),
    )
    out_specs = (
        P(None, MODE),
        P(None, MODE),
        P(None, MODE),
        P(MODE, None, SPACE),
        P(MODE, None, SPACE),
    )
    return jax.shard_map(local, mesh=fine, in_specs=in_specs, out_specs=out_specs, check_vma=False)
```

```python
import jax
import jax.numpy as jnp
from jax import lax
from jax.experimental import pallas as pl
from jax.experimental.pallas import tpu as pltpu
from jax.sharding import Mesh, PartitionSpec as P

SPACE = ("y", "zl")
MODE = ("x", "zh", "c")
R, M, C = 64, 32, 128
F32, BF16 = jnp.float32, jnp.bfloat16
VM = pl.BlockSpec(memory_space=pltpu.VMEM)
SM = pl.BlockSpec(memory_space=pltpu.SMEM)


def shifted(value, axis, step):
    n = lax.axis_size(axis)
    return lax.ppermute(value, axis, [(i, (i + step) % n) for i in range(n)])


def select_table(material, tables_ref, which):
    value = jnp.zeros(material.shape, F32)
    for level in range(tables_ref.shape[1]):
        value = jnp.where(material == level, tables_ref[which, level], value)
    return value


def edges_kernel(u_ref, mat_ref, first_ref, last_ref, sent_ref, mat):
    mat[...] = mat_ref[...].astype(F32)
    sent_ref[0:R] = u_ref[...]
    sent_ref[R : R + 2] = jnp.zeros((2, M, C), BF16)
    pair = lax.broadcasted_iota(jnp.int32, (8, C), 1) // 2
    firsts, lasts = [], []
    for m in range(0, M + 8, 8):
        first = last = jnp.zeros((8, C), F32)
        for r in range(R):
            v = u_ref[r, m : m + 8, :].astype(F32) if m < M else jnp.broadcast_to(mat[r : r + 1, :], (8, C))
            first = jnp.where(pair == r, pltpu.roll(v, 2 * r, 1), first)
            last = jnp.where(pair == r, pltpu.roll(v, (2 * r + 2) % C, 1), last)
        firsts.append(first)
        lasts.append(last)
    first_ref[...] = jnp.concatenate(firsts, axis=0).astype(BF16)
    last_ref[...] = jnp.concatenate(lasts, axis=0).astype(BF16)


def edges(u, material):
    return pl.pallas_call(
        edges_kernel,
        out_shape=[jax.ShapeDtypeStruct((M + 8, C), BF16)] * 2 + [jax.ShapeDtypeStruct((R + 2, M, C), BF16)],
        in_specs=[VM, VM],
        out_specs=[VM] * 3,
        scratch_shapes=[pltpu.VMEM((R, C), F32)],
        cost_estimate=pl.CostEstimate(flops=10**6, bytes_accessed=10**6, transcendentals=0),
    )(u, material)


def fields_kernel(mat_ref, left_ref, right_ref, tables_ref, f_ref, kx, ky, rho, dd):
    material = mat_ref[...]
    kx[...] = jnp.zeros(kx.shape, F32)
    kx[8 : 8 + R, :] = select_table(material, tables_ref, 1)
    ky[...] = select_table(material, tables_ref, 2)
    rho[...] = select_table(material, tables_ref, 0)
    dd[...] = select_table(material, tables_ref, 3)
    lane = lax.broadcasted_iota(jnp.int32, (1, C), 1)
    space = lax.axis_index("y") * 4 + lax.axis_index("zl")
    left = select_table(left_ref[M : M + 8, :].astype(F32), tables_ref, 2)
    left = jnp.where(space > 0, left, 0.0)
    right = select_table(right_ref[M : M + 8, :].astype(F32), tables_ref, 2)
    right = jnp.where(space < 31, right, 0.0)

    for r in range(R):
        k = ky[r : r + 1, :]
        kl = pltpu.roll(left, C - 1 - 2 * r, 1)[0:1]
        kr = pltpu.roll(right, C - 1 - 2 * r, 1)[0:1]
        k8 = jnp.broadcast_to(k, (8, C))
        south = jnp.where(lane == 0, kl, pltpu.roll(k8, 1, 1)[0:1])
        north = jnp.where(lane == C - 1, kr, pltpu.roll(k8, C - 1, 1)[0:1])
        kc = kx[r + 8 : r + 9, :]
        fe = 0.5 * (kc + kx[r + 9 : r + 10, :])
        fw = 0.5 * (kc + kx[r + 7 : r + 8, :])
        fn = 0.5 * (k + north)
        fs = 0.5 * (k + south)
        rr = rho[r : r + 1, :]
        rows = [rr * (2.0 / 3.0), rr * (1.0 / 12.0), fe + fw + fn + fs, fe, fw, fn, fs, dd[r : r + 1, :]]
        f_ref[r] = jnp.concatenate(rows, axis=0)


def fields(material, left, right, tables):
    return pl.pallas_call(
        fields_kernel,
        out_shape=jax.ShapeDtypeStruct((R, 8, C), F32),
        in_specs=[VM, VM, VM, SM],
        out_specs=VM,
        scratch_shapes=[pltpu.VMEM((R + 16, C), F32)] + [pltpu.VMEM((R, C), F32)] * 3,
        cost_estimate=pl.CostEstimate(flops=10**6, bytes_accessed=10**6, transcendentals=0),
    )(material, left, right, tables)


PIECE = 3 * M // 8
PANEL_FLOPS = 3 * 10**9
ROWS = 8


def panel_kernel(with_images, u_ref, f_ref, *rest):
    olds, rest = rest[:2], rest[2:]
    if with_images:
        half_ref, img, mass_ref, stiff_ref, us, s1, s2, q, acc = rest
    else:
        half_ref, img, us, s1, s2, q, acc = rest
    zero = jnp.zeros((M, C), F32)
    for r in (0, 1, R + 2, R + 3):
        us[r] = zero
    s1[0] = zero
    s1[R + 1] = zero
    lane = lax.broadcasted_iota(jnp.int32, (1, C), 1)
    left = u_ref[R].astype(F32)
    right = u_ref[R + 1].astype(F32)
    first = jnp.where(lane % 2 == 0, right, left)
    right = pltpu.roll(right, C - 2, 1)
    second = [jnp.where((lane // 2) % 2 == p, left, right) for p in (0, 1)]

    for r in range(R):
        u = u_ref[r].astype(F32)
        h1 = pltpu.roll(first, C - 1 - 2 * r, 1)
        h2 = pltpu.roll(second[r % 2], (C - 2 * r) % C, 1)
        south = jnp.where(lane == 0, h1, pltpu.roll(u, 1, 1))
        south2 = jnp.where(lane < 2, h2, pltpu.roll(u, 2, 1))
        north = jnp.where(lane == C - 1, h1, pltpu.roll(u, C - 1, 1))
        north2 = jnp.where(lane >= C - 2, h2, pltpu.roll(u, C - 2, 1))
        us[r + 2] = u
        s1[r + 1] = south + north
        s2[r] = south2 + north2
        q[r] = f_ref[r, 5:6, :] * north + f_ref[r, 6:7, :] * south

    acc[...] = jnp.zeros(acc.shape, F32)

    def rows(step, _):
        base = step * ROWS
        for j in range(ROWS):
            r = base + j
            u, east, west = us[r + 2], us[r + 3], us[r + 1]
            near = (east + west) + s1[r + 1]
            mass = f_ref[r, 0:1, :] * u + f_ref[r, 1:2, :] * near
            membrane = f_ref[r, 2:3, :] * u - f_ref[r, 3:4, :] * east - f_ref[r, 4:5, :] * west - q[r]
            far = (us[r + 4] + us[r]) + s2[r]
            diagonal = s1[r] + s1[r + 2]
            bending = f_ref[r, 7:8, :] * (20.0 * u - 8.0 * near + 2.0 * diagonal + far)
            for i, v in enumerate((mass, membrane, bending)):
                hi = v.astype(BF16)
                lo = (v - hi.astype(F32)).astype(BF16)
                img[step, M * i : M * i + M, C * j : C * j + C] = hi
                img[step, M * (i + 3) : M * (i + 3) + M, C * j : C * j + C] = lo
            if with_images:
                mass_ref[r] = mass.astype(BF16)
                stiff_ref[r] = (membrane + bending).astype(BF16)
        wide = [jnp.concatenate([o[base + j] for j in range(ROWS)], axis=1) for o in olds]
        acc[...] += lax.dot_general(
            img[step], jnp.concatenate(wide, axis=0), (((1,), (1,)), ((), ())), preferred_element_type=F32
        )
        return 0

    for step in range(R // ROWS):
        rows(step, 0)
    half_ref[...] = acc[0 : 3 * M] + acc[3 * M : 6 * M]


def panel(u, f, olds, with_images):
    outs = [
        jax.ShapeDtypeStruct((3 * M, 2 * M), F32),
        jax.ShapeDtypeStruct((R // ROWS, 6 * M, ROWS * C), BF16),
    ]
    outs += [jax.ShapeDtypeStruct((R, M, C), BF16)] * (2 if with_images else 0)
    return pl.pallas_call(
        lambda *refs: panel_kernel(with_images, *refs),
        out_shape=outs,
        in_specs=[VM] * 4,
        out_specs=[VM] * len(outs),
        scratch_shapes=[
            pltpu.VMEM((R + 4, M, C), F32),
            pltpu.VMEM((R + 2, M, C), F32),
            pltpu.VMEM((R, M, C), F32),
            pltpu.VMEM((R, M, C), F32),
            pltpu.VMEM((6 * M, 2 * M), F32),
        ],
        compiler_params=pltpu.CompilerParams(vmem_limit_bytes=20 * 2**20),
        cost_estimate=pl.CostEstimate(flops=PANEL_FLOPS, bytes_accessed=4 * 10**6, transcendentals=0),
    )(u, f, *olds)


def rest_kernel(*refs):
    halves, terms, olds, out_ref, acc = refs[:4], refs[4:8], refs[8:10], refs[10], refs[11]
    for step in range(R // ROWS):
        base = step * ROWS
        wide = [jnp.concatenate([o[base + j] for j in range(ROWS)], axis=1) for o in olds]
        wide = jnp.concatenate(wide, axis=0)
        for d in range(4):
            part = lax.dot_general(terms[d][step], wide, (((1,), (1,)), ((), ())), preferred_element_type=F32)
            acc[d] = part if step == 0 else acc[d] + part
    x, zh, c = lax.axis_index("x"), lax.axis_index("zh"), lax.axis_index("c")
    lane = lax.broadcasted_iota(jnp.int32, (1, 4 * M), 1)
    for d in range(4):
        v = jnp.concatenate([halves[d][...], acc[d, 0 : 3 * M] + acc[d, 3 * M : 6 * M]], axis=1)
        v = pltpu.roll(v, zh * 64, 1)
        swapped = jnp.where(lane % 64 < 32, pltpu.roll(v, 96, 1), pltpu.roll(v, 32, 1))
        v = jnp.where(c == 1, swapped, v)
        chip = lax.rem(x + d, 4)
        for k in range(4):

            @pl.when(chip == k)
            def _():
                for i in range(8):
                    out_ref[i, PIECE * k : PIECE * k + PIECE] = v[PIECE * i : PIECE * i + PIECE]


def rest(halves, terms, olds):
    operands = (*halves, *terms, *olds)
    return pl.pallas_call(
        rest_kernel,
        out_shape=jax.ShapeDtypeStruct((8, 4 * PIECE, 4 * M), F32),
        in_specs=[VM] * len(operands),
        out_specs=VM,
        scratch_shapes=[pltpu.VMEM((4, 6 * M, 2 * M), F32)],
        compiler_params=pltpu.CompilerParams(vmem_limit_bytes=20 * 2**20),
        cost_estimate=pl.CostEstimate(flops=3 * 10**9, bytes_accessed=14 * 10**6, transcendentals=0),
    )(*operands)


def local(old_modes, new_modes, material, density, memb_x, memb_y, bend_table):
    tables = jnp.stack([density, memb_x.astype(F32), memb_y.astype(F32), bend_table])
    first, last, sent = edges(new_modes.transpose(1, 0, 2), material)
    old = old_modes.transpose(1, 0, 2)
    n = 32
    left = lax.ppermute(last, SPACE, [(i, i + 1) for i in range(n - 1)])
    right = lax.ppermute(first, SPACE, [(i + 1, i) for i in range(n - 1)])
    left, right, far, tables = lax.optimization_barrier((left, right, old, tables))
    other = shifted(far, "zh", 1)
    own = lax.dynamic_update_slice(sent, jnp.stack([left[:M], right[:M]]), (R, 0, 0))
    panels = [own] + [shifted(own, "x", -d) for d in (1, 2, 3)]
    f = fields(material, left, right, tables)
    olds = (old, shifted(old, "c", 1))
    halves, terms = [None] * 4, [None] * 4
    halves[0], terms[0], mass, stiff = panel(own, f, olds, True)
    halves[0], other, panels[1], panels[3] = lax.optimization_barrier((halves[0], other, panels[1], panels[3]))
    other_core = shifted(other, "c", 1)
    for d in (1, 3, 2):
        if d == 2:
            halves[1], panels[2] = lax.optimization_barrier((halves[1], panels[2]))
        halves[d], terms[d] = panel(panels[d], f, olds, False)
    parts = rest(halves, terms, (other, other_core))
    parts = jnp.sum(lax.all_to_all(parts, "y", 0, 0), axis=0).reshape(4, 1, PIECE, 4 * M)
    parts = jnp.broadcast_to(parts, (4, 4, PIECE, 4 * M)).reshape(16, PIECE, 4 * M)
    parts = lax.all_to_all(parts, ("x", "zl"), 0, 0).reshape(4, 4, PIECE, 4 * M)
    parts = jnp.sum(parts, axis=1).reshape(1, 4 * PIECE, 4 * M)
    parts = lax.all_to_all(jnp.broadcast_to(parts, (8, 4 * PIECE, 4 * M)), "y", 0, 0)
    area = 1.0 / (R * C * n)
    total = parts.reshape(8, 4, PIECE, 4 * M).transpose(0, 2, 1, 3).reshape(3, M, 16 * M) * area
    return (*[total[i].T for i in range(3)], mass.transpose(1, 0, 2), stiff.transpose(1, 0, 2))


def solution(mesh):
    fine = Mesh(mesh.devices.reshape(8, 4, 4, 2, 2), ("y", "zl", "x", "zh", "c"))
    in_specs = (
        P(MODE, None, SPACE),
        P(MODE, None, SPACE),
        P(None, SPACE),
        P(),
        P(),
        P(),
        P(),
    )
    out_specs = (
        P(None, MODE),
        P(None, MODE),
        P(None, MODE),
        P(MODE, None, SPACE),
        P(MODE, None, SPACE),
    )
    return jax.shard_map(local, mesh=fine, in_specs=in_specs, out_specs=out_specs, check_vma=False)
```

```python
import jax
import jax.numpy as jnp
from jax import lax
from jax.experimental import pallas as pl
from jax.experimental.pallas import tpu as pltpu
from jax.sharding import Mesh, PartitionSpec as P

SPACE = ("y", "zl")
MODE = ("x", "zh", "c")
R, M, C = 64, 32, 128
F32, BF16 = jnp.float32, jnp.bfloat16
VM = pl.BlockSpec(memory_space=pltpu.VMEM)
SM = pl.BlockSpec(memory_space=pltpu.SMEM)


def shifted(value, axis, step):
    n = lax.axis_size(axis)
    return lax.ppermute(value, axis, [(i, (i + step) % n) for i in range(n)])


def select_table(material, tables_ref, which):
    value = jnp.zeros(material.shape, F32)
    for level in range(tables_ref.shape[1]):
        value = jnp.where(material == level, tables_ref[which, level], value)
    return value


def edges_kernel(u_ref, mat_ref, first_ref, last_ref, sent_ref, mat):
    mat[...] = mat_ref[...].astype(F32)
    sent_ref[0:R] = u_ref[...]
    sent_ref[R : R + 2] = jnp.zeros((2, M, C), BF16)
    pair = lax.broadcasted_iota(jnp.int32, (8, C), 1) // 2
    firsts, lasts = [], []
    for m in range(0, M + 8, 8):
        first = last = jnp.zeros((8, C), F32)
        for r in range(R):
            v = u_ref[r, m : m + 8, :].astype(F32) if m < M else jnp.broadcast_to(mat[r : r + 1, :], (8, C))
            first = jnp.where(pair == r, pltpu.roll(v, 2 * r, 1), first)
            last = jnp.where(pair == r, pltpu.roll(v, (2 * r + 2) % C, 1), last)
        firsts.append(first)
        lasts.append(last)
    first_ref[...] = jnp.concatenate(firsts, axis=0).astype(BF16)
    last_ref[...] = jnp.concatenate(lasts, axis=0).astype(BF16)


def edges(u, material):
    return pl.pallas_call(
        edges_kernel,
        out_shape=[jax.ShapeDtypeStruct((M + 8, C), BF16)] * 2 + [jax.ShapeDtypeStruct((R + 2, M, C), BF16)],
        in_specs=[VM, VM],
        out_specs=[VM] * 3,
        scratch_shapes=[pltpu.VMEM((R, C), F32)],
        cost_estimate=pl.CostEstimate(flops=10**6, bytes_accessed=10**6, transcendentals=0),
    )(u, material)


def fields_kernel(mat_ref, left_ref, right_ref, tables_ref, f_ref, kx, ky, rho, dd):
    material = mat_ref[...]
    kx[...] = jnp.zeros(kx.shape, F32)
    kx[8 : 8 + R, :] = select_table(material, tables_ref, 1)
    ky[...] = select_table(material, tables_ref, 2)
    rho[...] = select_table(material, tables_ref, 0)
    dd[...] = select_table(material, tables_ref, 3)
    lane = lax.broadcasted_iota(jnp.int32, (1, C), 1)
    space = lax.axis_index("y") * 4 + lax.axis_index("zl")
    left = select_table(left_ref[M : M + 8, :].astype(F32), tables_ref, 2)
    left = jnp.where(space > 0, left, 0.0)
    right = select_table(right_ref[M : M + 8, :].astype(F32), tables_ref, 2)
    right = jnp.where(space < 31, right, 0.0)

    for r in range(R):
        k = ky[r : r + 1, :]
        kl = pltpu.roll(left, C - 1 - 2 * r, 1)[0:1]
        kr = pltpu.roll(right, C - 1 - 2 * r, 1)[0:1]
        k8 = jnp.broadcast_to(k, (8, C))
        south = jnp.where(lane == 0, kl, pltpu.roll(k8, 1, 1)[0:1])
        north = jnp.where(lane == C - 1, kr, pltpu.roll(k8, C - 1, 1)[0:1])
        kc = kx[r + 8 : r + 9, :]
        fe = 0.5 * (kc + kx[r + 9 : r + 10, :])
        fw = 0.5 * (kc + kx[r + 7 : r + 8, :])
        fn = 0.5 * (k + north)
        fs = 0.5 * (k + south)
        rr = rho[r : r + 1, :]
        rows = [rr * (2.0 / 3.0), rr * (1.0 / 12.0), fe + fw + fn + fs, fe, fw, fn, fs, dd[r : r + 1, :]]
        f_ref[r] = jnp.concatenate(rows, axis=0)


def fields(material, left, right, tables):
    return pl.pallas_call(
        fields_kernel,
        out_shape=jax.ShapeDtypeStruct((R, 8, C), F32),
        in_specs=[VM, VM, VM, SM],
        out_specs=VM,
        scratch_shapes=[pltpu.VMEM((R + 16, C), F32)] + [pltpu.VMEM((R, C), F32)] * 3,
        cost_estimate=pl.CostEstimate(flops=10**6, bytes_accessed=10**6, transcendentals=0),
    )(material, left, right, tables)


PIECE = 3 * M // 8
PANEL_FLOPS = 3 * 10**9
ROWS = 8


def panel_kernel(with_images, u_ref, f_ref, *rest):
    olds, rest = rest[:2], rest[2:]
    if with_images:
        half_ref, img, mass_ref, stiff_ref, us, s1, s2, q, acc = rest
    else:
        half_ref, img, us, s1, s2, q, acc = rest
    zero = jnp.zeros((M, C), F32)
    for r in (0, 1, R + 2, R + 3):
        us[r] = zero
    s1[0] = zero
    s1[R + 1] = zero
    lane = lax.broadcasted_iota(jnp.int32, (1, C), 1)
    left = u_ref[R].astype(F32)
    right = u_ref[R + 1].astype(F32)
    first = jnp.where(lane % 2 == 0, right, left)
    right = pltpu.roll(right, C - 2, 1)
    second = [jnp.where((lane // 2) % 2 == p, left, right) for p in (0, 1)]

    for r in range(R):
        u = u_ref[r].astype(F32)
        h1 = pltpu.roll(first, C - 1 - 2 * r, 1)
        h2 = pltpu.roll(second[r % 2], (C - 2 * r) % C, 1)
        south = jnp.where(lane == 0, h1, pltpu.roll(u, 1, 1))
        south2 = jnp.where(lane < 2, h2, pltpu.roll(u, 2, 1))
        north = jnp.where(lane == C - 1, h1, pltpu.roll(u, C - 1, 1))
        north2 = jnp.where(lane >= C - 2, h2, pltpu.roll(u, C - 2, 1))
        us[r + 2] = u
        s1[r + 1] = south + north
        s2[r] = south2 + north2
        q[r] = f_ref[r, 5:6, :] * north + f_ref[r, 6:7, :] * south

    acc[...] = jnp.zeros(acc.shape, F32)

    def rows(step, _):
        base = step * ROWS
        for j in range(ROWS):
            r = base + j
            u, east, west = us[r + 2], us[r + 3], us[r + 1]
            near = (east + west) + s1[r + 1]
            mass = f_ref[r, 0:1, :] * u + f_ref[r, 1:2, :] * near
            membrane = f_ref[r, 2:3, :] * u - f_ref[r, 3:4, :] * east - f_ref[r, 4:5, :] * west - q[r]
            far = (us[r + 4] + us[r]) + s2[r]
            diagonal = s1[r] + s1[r + 2]
            bending = f_ref[r, 7:8, :] * (20.0 * u - 8.0 * near + 2.0 * diagonal + far)
            for i, v in enumerate((mass, membrane, bending)):
                hi = v.astype(BF16)
                lo = (v - hi.astype(F32)).astype(BF16)
                img[step, M * i : M * i + M, C * j : C * j + C] = hi
                img[step, M * (i + 3) : M * (i + 3) + M, C * j : C * j + C] = lo
            if with_images:
                mass_ref[r] = mass.astype(BF16)
                stiff_ref[r] = (membrane + bending).astype(BF16)
        wide = [jnp.concatenate([o[base + j] for j in range(ROWS)], axis=1) for o in olds]
        acc[...] += lax.dot_general(
            img[step], jnp.concatenate(wide, axis=0), (((1,), (1,)), ((), ())), preferred_element_type=F32
        )
        return 0

    for step in range(R // ROWS):
        rows(step, 0)
    half_ref[...] = acc[0 : 3 * M] + acc[3 * M : 6 * M]


def panel(u, f, olds, with_images):
    outs = [
        jax.ShapeDtypeStruct((3 * M, 2 * M), F32),
        jax.ShapeDtypeStruct((R // ROWS, 6 * M, ROWS * C), BF16),
    ]
    outs += [jax.ShapeDtypeStruct((R, M, C), BF16)] * (2 if with_images else 0)
    return pl.pallas_call(
        lambda *refs: panel_kernel(with_images, *refs),
        out_shape=outs,
        in_specs=[VM] * 4,
        out_specs=[VM] * len(outs),
        scratch_shapes=[
            pltpu.VMEM((R + 4, M, C), F32),
            pltpu.VMEM((R + 2, M, C), F32),
            pltpu.VMEM((R, M, C), F32),
            pltpu.VMEM((R, M, C), F32),
            pltpu.VMEM((6 * M, 2 * M), F32),
        ],
        compiler_params=pltpu.CompilerParams(vmem_limit_bytes=20 * 2**20),
        cost_estimate=pl.CostEstimate(flops=PANEL_FLOPS, bytes_accessed=4 * 10**6, transcendentals=0),
    )(u, f, *olds)


def rest_kernel(*refs):
    halves, terms, olds, out_ref, acc = refs[:4], refs[4:8], refs[8:10], refs[10], refs[11]
    for step in range(R // ROWS):
        base = step * ROWS
        wide = [jnp.concatenate([o[base + j] for j in range(ROWS)], axis=1) for o in olds]
        wide = jnp.concatenate(wide, axis=0)
        for d in range(4):
            part = lax.dot_general(terms[d][step], wide, (((1,), (1,)), ((), ())), preferred_element_type=F32)
            acc[d] = part if step == 0 else acc[d] + part
    x, zh, c = lax.axis_index("x"), lax.axis_index("zh"), lax.axis_index("c")
    lane = lax.broadcasted_iota(jnp.int32, (1, 4 * M), 1)
    for d in range(4):
        v = jnp.concatenate([halves[d][...], acc[d, 0 : 3 * M] + acc[d, 3 * M : 6 * M]], axis=1)
        v = pltpu.roll(v, zh * 64, 1)
        swapped = jnp.where(lane % 64 < 32, pltpu.roll(v, 96, 1), pltpu.roll(v, 32, 1))
        v = jnp.where(c == 1, swapped, v)
        chip = lax.rem(x + d, 4)
        for k in range(4):

            @pl.when(chip == k)
            def _():
                for i in range(8):
                    out_ref[i, PIECE * k : PIECE * k + PIECE] = v[PIECE * i : PIECE * i + PIECE]


def rest(halves, terms, olds):
    operands = (*halves, *terms, *olds)
    return pl.pallas_call(
        rest_kernel,
        out_shape=jax.ShapeDtypeStruct((8, 4 * PIECE, 4 * M), F32),
        in_specs=[VM] * len(operands),
        out_specs=VM,
        scratch_shapes=[pltpu.VMEM((4, 6 * M, 2 * M), F32)],
        compiler_params=pltpu.CompilerParams(vmem_limit_bytes=20 * 2**20),
        cost_estimate=pl.CostEstimate(flops=3 * 10**9, bytes_accessed=14 * 10**6, transcendentals=0),
    )(*operands)


def local(old_modes, new_modes, material, density, memb_x, memb_y, bend_table):
    tables = jnp.stack([density, memb_x.astype(F32), memb_y.astype(F32), bend_table])
    first, last, sent = edges(new_modes.transpose(1, 0, 2), material)
    first, last, old_modes = lax.optimization_barrier((first, last, old_modes))
    old = old_modes.transpose(1, 0, 2)
    other = shifted(old, "zh", 1)
    n = 32
    left = lax.ppermute(last, SPACE, [(i, i + 1) for i in range(n - 1)])
    right = lax.ppermute(first, SPACE, [(i + 1, i) for i in range(n - 1)])
    left, right, near, tables = lax.optimization_barrier((left, right, old, tables))
    own = lax.dynamic_update_slice(sent, jnp.stack([left[:M], right[:M]]), (R, 0, 0))
    panels = [own] + [shifted(own, "x", -d) for d in (1, 2, 3)]
    f = fields(material, left, right, tables)
    olds = (old, shifted(near, "c", 1))
    halves, terms = [None] * 4, [None] * 4
    f, other = lax.optimization_barrier((f, other))
    other_core = shifted(other, "c", 1)
    halves[0], terms[0], mass, stiff = panel(own, f, olds, True)
    halves[0], panels[1], panels[3] = lax.optimization_barrier((halves[0], panels[1], panels[3]))
    for d in (1, 3, 2):
        if d == 2:
            halves[3], panels[2] = lax.optimization_barrier((halves[3], panels[2]))
        halves[d], terms[d] = panel(panels[d], f, olds, False)
    parts = rest(halves, terms, (other, other_core))
    parts = jnp.sum(lax.all_to_all(parts, "y", 0, 0), axis=0).reshape(4, 1, PIECE, 4 * M)
    parts = jnp.broadcast_to(parts, (4, 4, PIECE, 4 * M)).reshape(16, PIECE, 4 * M)
    parts = lax.all_to_all(parts, ("x", "zl"), 0, 0).reshape(4, 4, PIECE, 4 * M)
    parts = jnp.sum(parts, axis=1).reshape(1, 4 * PIECE, 4 * M)
    parts = lax.all_to_all(jnp.broadcast_to(parts, (8, 4 * PIECE, 4 * M)), "y", 0, 0)
    area = 1.0 / (R * C * n)
    total = parts.reshape(8, 4, PIECE, 4 * M).transpose(0, 2, 1, 3).reshape(3, M, 16 * M) * area
    return (*[total[i].T for i in range(3)], mass.transpose(1, 0, 2), stiff.transpose(1, 0, 2))


def solution(mesh):
    fine = Mesh(mesh.devices.reshape(8, 4, 4, 2, 2), ("y", "zl", "x", "zh", "c"))
    in_specs = (
        P(MODE, None, SPACE),
        P(MODE, None, SPACE),
        P(None, SPACE),
        P(),
        P(),
        P(),
        P(),
    )
    out_specs = (
        P(None, MODE),
        P(None, MODE),
        P(None, MODE),
        P(MODE, None, SPACE),
        P(MODE, None, SPACE),
    )
    return jax.shard_map(local, mesh=fine, in_specs=in_specs, out_specs=out_specs, check_vma=False)
```

```python
import jax
import jax.numpy as jnp
from jax import lax
from jax.experimental import pallas as pl
from jax.experimental.pallas import tpu as pltpu
from jax.sharding import Mesh, PartitionSpec as P

SPACE = ("y", "zl")
MODE = ("x", "zh", "c")
R, M, C = 64, 32, 128
F32, BF16 = jnp.float32, jnp.bfloat16
VM = pl.BlockSpec(memory_space=pltpu.VMEM)
SM = pl.BlockSpec(memory_space=pltpu.SMEM)


def shifted(value, axis, step):
    n = lax.axis_size(axis)
    return lax.ppermute(value, axis, [(i, (i + step) % n) for i in range(n)])


def select_table(material, values):
    value = jnp.zeros(material.shape, F32)
    for level, entry in enumerate(values):
        value = jnp.where(material == level, entry, value)
    return value


def edges_kernel(u_ref, mat_ref, first_ref, last_ref, sent_ref, mat):
    mat[...] = mat_ref[...].astype(F32)
    sent_ref[0:R] = u_ref[...]
    sent_ref[R : R + 2] = jnp.zeros((2, M, C), BF16)
    pair = lax.broadcasted_iota(jnp.int32, (8, C), 1) // 2
    firsts, lasts = [], []
    for m in range(0, M + 8, 8):
        first = last = jnp.zeros((8, C), F32)
        for r in range(R):
            v = u_ref[r, m : m + 8, :].astype(F32) if m < M else jnp.broadcast_to(mat[r : r + 1, :], (8, C))
            first = jnp.where(pair == r, pltpu.roll(v, 2 * r, 1), first)
            last = jnp.where(pair == r, pltpu.roll(v, (2 * r + 2) % C, 1), last)
        firsts.append(first)
        lasts.append(last)
    first_ref[...] = jnp.concatenate(firsts, axis=0).astype(BF16)
    last_ref[...] = jnp.concatenate(lasts, axis=0).astype(BF16)


def edges(u, material):
    return pl.pallas_call(
        edges_kernel,
        out_shape=[jax.ShapeDtypeStruct((M + 8, C), BF16)] * 2 + [jax.ShapeDtypeStruct((R + 2, M, C), BF16)],
        in_specs=[VM, VM],
        out_specs=[VM] * 3,
        scratch_shapes=[pltpu.VMEM((R, C), F32)],
        cost_estimate=pl.CostEstimate(flops=10**6, bytes_accessed=10**6, transcendentals=0),
    )(u, material)


def fields_kernel(mat_ref, left_ref, right_ref, rho_ref, mx_ref, my_ref, dd_ref, f_ref, kx, ky, rho, dd):
    material = mat_ref[...]
    count = rho_ref.shape[0]
    densities, bends = ([ref[i] for i in range(count)] for ref in (rho_ref, dd_ref))
    mx, my = ([ref[:, i : i + 1].astype(F32) for i in range(count)] for ref in (mx_ref, my_ref))
    kx[...] = jnp.zeros(kx.shape, F32)
    kx[8 : 8 + R, :] = select_table(material, mx)
    ky[...] = select_table(material, my)
    rho[...] = select_table(material, densities)
    dd[...] = select_table(material, bends)
    lane = lax.broadcasted_iota(jnp.int32, (1, C), 1)
    space = lax.axis_index("y") * 4 + lax.axis_index("zl")
    left = select_table(left_ref[M : M + 8, :].astype(F32), my)
    left = jnp.where(space > 0, left, 0.0)
    right = select_table(right_ref[M : M + 8, :].astype(F32), my)
    right = jnp.where(space < 31, right, 0.0)

    for r in range(R):
        k = ky[r : r + 1, :]
        kl = pltpu.roll(left, C - 1 - 2 * r, 1)[0:1]
        kr = pltpu.roll(right, C - 1 - 2 * r, 1)[0:1]
        k8 = jnp.broadcast_to(k, (8, C))
        south = jnp.where(lane == 0, kl, pltpu.roll(k8, 1, 1)[0:1])
        north = jnp.where(lane == C - 1, kr, pltpu.roll(k8, C - 1, 1)[0:1])
        kc = kx[r + 8 : r + 9, :]
        fe = 0.5 * (kc + kx[r + 9 : r + 10, :])
        fw = 0.5 * (kc + kx[r + 7 : r + 8, :])
        fn = 0.5 * (k + north)
        fs = 0.5 * (k + south)
        rr = rho[r : r + 1, :]
        rows = [rr * (2.0 / 3.0), rr * (1.0 / 12.0), fe + fw + fn + fs, fe, fw, fn, fs, dd[r : r + 1, :]]
        f_ref[r] = jnp.concatenate(rows, axis=0)


def fields(material, left, right, density, memb_x, memb_y, bend_table):
    return pl.pallas_call(
        fields_kernel,
        out_shape=jax.ShapeDtypeStruct((R, 8, C), F32),
        in_specs=[VM, VM, VM, SM, VM, VM, SM],
        out_specs=VM,
        scratch_shapes=[pltpu.VMEM((R + 16, C), F32)] + [pltpu.VMEM((R, C), F32)] * 3,
        cost_estimate=pl.CostEstimate(flops=10**6, bytes_accessed=10**6, transcendentals=0),
    )(material, left, right, density, memb_x[None], memb_y[None], bend_table)


PIECE = 3 * M // 8
ROWS = 8


def panel_kernel(d, u_ref, f_ref, *rest):
    with_images = d == 0
    olds, rest = rest[:4], rest[4 if d == 0 else 5 :]
    if with_images:
        out_ref, mass_ref, stiff_ref, us, s1, s2, q, img, acc = rest
    else:
        out_ref, us, s1, s2, q, img, acc = rest
    zero = jnp.zeros((M, C), F32)
    for r in (0, 1, R + 2, R + 3):
        us[r] = zero
    s1[0] = zero
    s1[R + 1] = zero
    lane = lax.broadcasted_iota(jnp.int32, (1, C), 1)
    left = u_ref[R].astype(F32)
    right = u_ref[R + 1].astype(F32)
    first = jnp.where(lane % 2 == 0, right, left)
    right = pltpu.roll(right, C - 2, 1)
    second = [jnp.where((lane // 2) % 2 == p, left, right) for p in (0, 1)]

    for r in range(R):
        u = u_ref[r].astype(F32)
        h1 = pltpu.roll(first, C - 1 - 2 * r, 1)
        h2 = pltpu.roll(second[r % 2], (C - 2 * r) % C, 1)
        south = jnp.where(lane == 0, h1, pltpu.roll(u, 1, 1))
        south2 = jnp.where(lane < 2, h2, pltpu.roll(u, 2, 1))
        north = jnp.where(lane == C - 1, h1, pltpu.roll(u, C - 1, 1))
        north2 = jnp.where(lane >= C - 2, h2, pltpu.roll(u, C - 2, 1))
        us[r + 2] = u
        s1[r + 1] = south + north
        s2[r] = south2 + north2
        q[r] = f_ref[r, 5:6, :] * north + f_ref[r, 6:7, :] * south

    acc[...] = jnp.zeros(acc.shape, F32)

    def rows(step, _):
        base = step * ROWS
        for j in range(ROWS):
            r = base + j
            u, east, west = us[r + 2], us[r + 3], us[r + 1]
            near = (east + west) + s1[r + 1]
            mass = f_ref[r, 0:1, :] * u + f_ref[r, 1:2, :] * near
            membrane = f_ref[r, 2:3, :] * u - f_ref[r, 3:4, :] * east - f_ref[r, 4:5, :] * west - q[r]
            far = (us[r + 4] + us[r]) + s2[r]
            diagonal = s1[r] + s1[r + 2]
            bending = f_ref[r, 7:8, :] * (20.0 * u - 8.0 * near + 2.0 * diagonal + far)
            for i, v in enumerate((mass, membrane, bending)):
                hi = v.astype(BF16)
                lo = (v - hi.astype(F32)).astype(BF16)
                img[step % 2, M * i : M * i + M, C * j : C * j + C] = hi
                img[step % 2, M * (i + 3) : M * (i + 3) + M, C * j : C * j + C] = lo
            if with_images:
                mass_ref[r] = mass.astype(BF16)
                stiff_ref[r] = (membrane + bending).astype(BF16)
        wide = [jnp.concatenate([o[base + j] for j in range(ROWS)], axis=1) for o in olds]
        acc[...] += lax.dot_general(
            img[step % 2], jnp.concatenate(wide, axis=0), (((1,), (1,)), ((), ())), preferred_element_type=F32
        )
        return 0

    for step in range(R // ROWS):
        rows(step, 0)
    zh, c = lax.axis_index("zh"), lax.axis_index("c")
    v = pltpu.roll(acc[0 : 3 * M] + acc[3 * M : 6 * M], zh * 64, 1)
    lane = lax.broadcasted_iota(jnp.int32, (1, 4 * M), 1)
    swapped = jnp.where(lane % 64 < 32, pltpu.roll(v, 96, 1), pltpu.roll(v, 32, 1))
    v = jnp.where(c == 1, swapped, v)
    chip = lax.rem(lax.axis_index("x") + d, 4)
    for k in range(4):

        @pl.when(chip == k)
        def _():
            for i in range(8):
                out_ref[i, PIECE * k : PIECE * k + PIECE] = v[PIECE * i : PIECE * i + PIECE]


def panel(d, u, f, olds, parts):
    outs = [jax.ShapeDtypeStruct((8, 4 * PIECE, 4 * M), F32)]
    outs += [jax.ShapeDtypeStruct((R, M, C), BF16)] * (2 if d == 0 else 0)
    operands = [u, f, *olds] + ([] if d == 0 else [parts])
    return pl.pallas_call(
        lambda *refs: panel_kernel(d, *refs),
        out_shape=outs,
        in_specs=[VM] * 6 + ([] if d == 0 else [pl.BlockSpec(memory_space=pl.ANY)]),
        out_specs=[VM] * len(outs),
        input_output_aliases={} if d == 0 else {6: 0},
        scratch_shapes=[
            pltpu.VMEM((R + 4, M, C), F32),
            pltpu.VMEM((R + 2, M, C), F32),
            pltpu.VMEM((R, M, C), F32),
            pltpu.VMEM((R, M, C), F32),
            pltpu.VMEM((2, 6 * M, ROWS * C), BF16),
            pltpu.VMEM((6 * M, 4 * M), F32),
        ],
        compiler_params=pltpu.CompilerParams(vmem_limit_bytes=16 * 2**20),
        cost_estimate=pl.CostEstimate(flops=4 * 10**8, bytes_accessed=4 * 10**6, transcendentals=0),
    )(*operands)


def local(old_modes, new_modes, material, density, memb_x, memb_y, bend_table):
    first, last, sent = edges(new_modes.transpose(1, 0, 2), material)
    first, last, old_modes = lax.optimization_barrier((first, last, old_modes))
    old = old_modes.transpose(1, 0, 2)
    other = shifted(old, "zh", 1)
    old_core = shifted(old, "c", 1)
    n = 32
    left = lax.ppermute(last, SPACE, [(i, i + 1) for i in range(n - 1)])
    right = lax.ppermute(first, SPACE, [(i + 1, i) for i in range(n - 1)])
    own = lax.dynamic_update_slice(sent, jnp.stack([left[:M], right[:M]]), (R, 0, 0))
    panels = [own] + [shifted(own, "x", -d) for d in (1, 2, 3)]
    f = fields(material, left, right, density, memb_x, memb_y, bend_table)
    f, other = lax.optimization_barrier((f, other))
    other_core = shifted(other, "c", 1)
    other_core, panels[1:] = lax.optimization_barrier((other_core, panels[1:]))
    olds = (old, old_core, other, other_core)
    parts, mass, stiff = panel(0, own, f, olds, None)
    for d in (1, 3, 2):
        (parts,) = panel(d, panels[d], f, olds, parts)
    parts = jnp.sum(lax.all_to_all(parts, "y", 0, 0), axis=0).reshape(4, 1, PIECE, 4 * M)
    parts = jnp.broadcast_to(parts, (4, 4, PIECE, 4 * M)).reshape(16, PIECE, 4 * M)
    parts = lax.all_to_all(parts, ("x", "zl"), 0, 0).reshape(4, 4, PIECE, 4 * M)
    parts = jnp.sum(parts, axis=1).reshape(1, 4 * PIECE, 4 * M)
    parts = lax.all_to_all(jnp.broadcast_to(parts, (8, 4 * PIECE, 4 * M)), "y", 0, 0)
    area = 1.0 / (R * C * n)
    total = parts.reshape(8, 4, PIECE, 4 * M).transpose(0, 2, 1, 3).reshape(3, M, 16 * M) * area
    return (*[total[i].T for i in range(3)], mass.transpose(1, 0, 2), stiff.transpose(1, 0, 2))


def solution(mesh):
    fine = Mesh(mesh.devices.reshape(8, 4, 4, 2, 2), ("y", "zl", "x", "zh", "c"))
    in_specs = (
        P(MODE, None, SPACE),
        P(MODE, None, SPACE),
        P(None, SPACE),
        P(),
        P(),
        P(),
        P(),
    )
    out_specs = (
        P(None, MODE),
        P(None, MODE),
        P(None, MODE),
        P(MODE, None, SPACE),
        P(MODE, None, SPACE),
    )
    return jax.shard_map(local, mesh=fine, in_specs=in_specs, out_specs=out_specs, check_vma=False)
```

```python
import jax
import jax.numpy as jnp
from jax import lax
from jax.experimental import pallas as pl
from jax.experimental.pallas import tpu as pltpu
from jax.experimental.layout import Layout, with_layout_constraint
from jax.sharding import Mesh, PartitionSpec as P

SPACE = ("y", "zl")
MODE = ("x", "zh", "c")
R, M, C = 64, 32, 128
F32, BF16 = jnp.float32, jnp.bfloat16
VM = pl.BlockSpec(memory_space=pltpu.VMEM)
SM = pl.BlockSpec(memory_space=pltpu.SMEM)


def shifted(value, axis, step):
    n = lax.axis_size(axis)
    return lax.ppermute(value, axis, [(i, (i + step) % n) for i in range(n)])


def select_table(material, values):
    value = jnp.zeros(material.shape, F32)
    for level, entry in enumerate(values):
        value = jnp.where(material == level, entry, value)
    return value


def edges_kernel(u_ref, mat_ref, first_ref, last_ref, sent_ref, mat):
    mat[...] = mat_ref[...].astype(F32)
    sent_ref[0:R] = u_ref[...]
    sent_ref[R : R + 2] = jnp.zeros((2, M, C), BF16)
    pair = lax.broadcasted_iota(jnp.int32, (8, C), 1) // 2
    firsts, lasts = [], []
    for m in range(0, M + 8, 8):
        first = last = jnp.zeros((8, C), F32)
        for r in range(R):
            v = u_ref[r, m : m + 8, :].astype(F32) if m < M else jnp.broadcast_to(mat[r : r + 1, :], (8, C))
            first = jnp.where(pair == r, pltpu.roll(v, 2 * r, 1), first)
            last = jnp.where(pair == r, pltpu.roll(v, (2 * r + 2) % C, 1), last)
        firsts.append(first)
        lasts.append(last)
    first_ref[...] = jnp.concatenate(firsts, axis=0).astype(BF16)
    last_ref[...] = jnp.concatenate(lasts, axis=0).astype(BF16)


def edges(u, material):
    return pl.pallas_call(
        edges_kernel,
        out_shape=[jax.ShapeDtypeStruct((M + 8, C), BF16)] * 2 + [jax.ShapeDtypeStruct((R + 2, M, C), BF16)],
        in_specs=[VM, VM],
        out_specs=[VM] * 3,
        scratch_shapes=[pltpu.VMEM((R, C), F32)],
        cost_estimate=pl.CostEstimate(flops=10**6, bytes_accessed=10**6, transcendentals=0),
    )(u, material)


def fields_kernel(mat_ref, left_ref, right_ref, rho_ref, mx_ref, my_ref, dd_ref, f_ref, kx, ky, rho, dd):
    material = mat_ref[...]
    count = rho_ref.shape[0]
    densities, bends = ([ref[i] for i in range(count)] for ref in (rho_ref, dd_ref))
    mx, my = ([ref[:, i : i + 1].astype(F32) for i in range(count)] for ref in (mx_ref, my_ref))
    kx[...] = jnp.zeros(kx.shape, F32)
    kx[8 : 8 + R, :] = select_table(material, mx)
    ky[...] = select_table(material, my)
    rho[...] = select_table(material, densities)
    dd[...] = select_table(material, bends)
    lane = lax.broadcasted_iota(jnp.int32, (1, C), 1)
    space = lax.axis_index("y") * 4 + lax.axis_index("zl")
    left = select_table(left_ref[M : M + 8, :].astype(F32), my)
    left = jnp.where(space > 0, left, 0.0)
    right = select_table(right_ref[M : M + 8, :].astype(F32), my)
    right = jnp.where(space < 31, right, 0.0)

    for r in range(R):
        k = ky[r : r + 1, :]
        kl = pltpu.roll(left, C - 1 - 2 * r, 1)[0:1]
        kr = pltpu.roll(right, C - 1 - 2 * r, 1)[0:1]
        k8 = jnp.broadcast_to(k, (8, C))
        south = jnp.where(lane == 0, kl, pltpu.roll(k8, 1, 1)[0:1])
        north = jnp.where(lane == C - 1, kr, pltpu.roll(k8, C - 1, 1)[0:1])
        kc = kx[r + 8 : r + 9, :]
        fe = 0.5 * (kc + kx[r + 9 : r + 10, :])
        fw = 0.5 * (kc + kx[r + 7 : r + 8, :])
        fn = 0.5 * (k + north)
        fs = 0.5 * (k + south)
        rr = rho[r : r + 1, :]
        rows = [rr * (2.0 / 3.0), rr * (1.0 / 12.0), fe + fw + fn + fs, fe, fw, fn, fs, dd[r : r + 1, :]]
        f_ref[r] = jnp.concatenate(rows, axis=0)


def fields(material, left, right, density, memb_x, memb_y, bend_table):
    return pl.pallas_call(
        fields_kernel,
        out_shape=jax.ShapeDtypeStruct((R, 8, C), F32),
        in_specs=[VM, VM, VM, SM, VM, VM, SM],
        out_specs=VM,
        scratch_shapes=[pltpu.VMEM((R + 16, C), F32)] + [pltpu.VMEM((R, C), F32)] * 3,
        cost_estimate=pl.CostEstimate(flops=10**6, bytes_accessed=10**6, transcendentals=0),
    )(material, left, right, density, memb_x[None], memb_y[None], bend_table)


PIECE = 3 * M // 8
ROWS = 8


def panel_kernel(d, u_ref, f_ref, *rest):
    if d == 0:
        img, mass_ref, stiff_ref, us, s1, s2, q = rest
    else:
        olds, own_ref = rest[:4], rest[4]
        out_ref, us, s1, s2, q, img, acc = rest[5:]
    zero = jnp.zeros((M, C), F32)
    for r in (0, 1, R + 2, R + 3):
        us[r] = zero
    s1[0] = zero
    s1[R + 1] = zero
    lane = lax.broadcasted_iota(jnp.int32, (1, C), 1)
    left = u_ref[R].astype(F32)
    right = u_ref[R + 1].astype(F32)
    first = jnp.where(lane % 2 == 0, right, left)
    right = pltpu.roll(right, C - 2, 1)
    second = [jnp.where((lane // 2) % 2 == p, left, right) for p in (0, 1)]

    for r in range(R):
        u = u_ref[r].astype(F32)
        h1 = pltpu.roll(first, C - 1 - 2 * r, 1)
        h2 = pltpu.roll(second[r % 2], (C - 2 * r) % C, 1)
        south = jnp.where(lane == 0, h1, pltpu.roll(u, 1, 1))
        south2 = jnp.where(lane < 2, h2, pltpu.roll(u, 2, 1))
        north = jnp.where(lane == C - 1, h1, pltpu.roll(u, C - 1, 1))
        north2 = jnp.where(lane >= C - 2, h2, pltpu.roll(u, C - 2, 1))
        us[r + 2] = u
        s1[r + 1] = south + north
        s2[r] = south2 + north2
        q[r] = f_ref[r, 5:6, :] * north + f_ref[r, 6:7, :] * south

    if d > 0:
        acc[...] = jnp.zeros(acc.shape, F32)

    def rows(step, slot):
        base = step * ROWS
        for j in range(ROWS):
            r = base + j
            u, east, west = us[r + 2], us[r + 3], us[r + 1]
            near = (east + west) + s1[r + 1]
            mass = f_ref[r, 0:1, :] * u + f_ref[r, 1:2, :] * near
            membrane = f_ref[r, 2:3, :] * u - f_ref[r, 3:4, :] * east - f_ref[r, 4:5, :] * west - q[r]
            far = (us[r + 4] + us[r]) + s2[r]
            diagonal = s1[r] + s1[r + 2]
            bending = f_ref[r, 7:8, :] * (20.0 * u - 8.0 * near + 2.0 * diagonal + far)
            for i, v in enumerate((mass, membrane, bending)):
                hi = v.astype(BF16)
                lo = (v - hi.astype(F32)).astype(BF16)
                img[slot, M * i : M * i + M, C * j : C * j + C] = hi
                img[slot, M * (i + 3) : M * (i + 3) + M, C * j : C * j + C] = lo
            if d == 0:
                mass_ref[r] = mass.astype(BF16)
                stiff_ref[r] = (membrane + bending).astype(BF16)
        if d == 0:
            return
        wide = [jnp.concatenate([o[base + j] for j in range(ROWS)], axis=1) for o in olds]
        wide = jnp.concatenate(wide, axis=0)
        dims = (((1,), (1,)), ((), ()))
        acc[0] += lax.dot_general(img[slot], wide, dims, preferred_element_type=F32)
        if d == 1:
            acc[1] += lax.dot_general(own_ref[step], wide, dims, preferred_element_type=F32)

    for step in range(R // ROWS):
        rows(step, step if d == 0 else step % 2)
    if d == 0:
        return
    zh, c = lax.axis_index("zh"), lax.axis_index("c")
    lane = lax.broadcasted_iota(jnp.int32, (1, 4 * M), 1)
    for i, away in enumerate((d, 0) if d == 1 else (d,)):
        v = pltpu.roll(acc[i, 0 : 3 * M] + acc[i, 3 * M : 6 * M], zh * 64, 1)
        swapped = jnp.where(lane % 64 < 32, pltpu.roll(v, 96, 1), pltpu.roll(v, 32, 1))
        v = jnp.where(c == 1, swapped, v)
        put(out_ref, v, lax.rem(lax.axis_index("x") + away, 4))


def put(out_ref, v, chip):
    for k in range(4):

        @pl.when(chip == k)
        def _():
            for i in range(8):
                out_ref[i, PIECE * k : PIECE * k + PIECE] = v[PIECE * i : PIECE * i + PIECE]


TERMS = (R // ROWS, 6 * M, ROWS * C)


def fields_scratch():
    shapes = ((R + 4, M, C), (R + 2, M, C), (R, M, C), (R, M, C))
    return [pltpu.VMEM(shape, F32) for shape in shapes]


def own_panel(u, f):
    return pl.pallas_call(
        lambda *refs: panel_kernel(0, *refs),
        out_shape=[jax.ShapeDtypeStruct(TERMS, BF16)] + [jax.ShapeDtypeStruct((R, M, C), BF16)] * 2,
        in_specs=[VM] * 2,
        out_specs=[VM] * 3,
        scratch_shapes=fields_scratch(),
        compiler_params=pltpu.CompilerParams(vmem_limit_bytes=20 * 2**20),
        cost_estimate=pl.CostEstimate(flops=4 * 10**8, bytes_accessed=4 * 10**6, transcendentals=0),
    )(u, f)


def panel(d, u, f, olds, extra):
    operands = [u, f, *olds, extra]
    return pl.pallas_call(
        lambda *refs: panel_kernel(d, *refs),
        out_shape=jax.ShapeDtypeStruct((8, 4 * PIECE, 4 * M), F32),
        in_specs=[VM] * 6 + [VM if d == 1 else pl.BlockSpec(memory_space=pl.ANY)],
        out_specs=VM,
        input_output_aliases={} if d == 1 else {6: 0},
        scratch_shapes=fields_scratch()
        + [pltpu.VMEM((2, 6 * M, ROWS * C), BF16), pltpu.VMEM((2 if d == 1 else 1, 6 * M, 4 * M), F32)],
        compiler_params=pltpu.CompilerParams(vmem_limit_bytes=20 * 2**20),
        cost_estimate=pl.CostEstimate(flops=4 * 10**8, bytes_accessed=4 * 10**6, transcendentals=0),
    )(*operands)


def local(old_modes, new_modes, material, density, memb_x, memb_y, bend_table):
    first, last, sent = edges(new_modes.transpose(1, 0, 2), material)
    first, last, old_modes = lax.optimization_barrier((first, last, old_modes))
    old = old_modes.transpose(1, 0, 2)
    other = shifted(old, "zh", 1)
    old_core = shifted(old, "c", 1)
    n = 32
    left = lax.ppermute(last, SPACE, [(i, i + 1) for i in range(n - 1)])
    right = lax.ppermute(first, SPACE, [(i + 1, i) for i in range(n - 1)])
    own = lax.dynamic_update_slice(sent, jnp.stack([left[:M], right[:M]]), (R, 0, 0))
    panels = [own] + [shifted(own, "x", -d) for d in (1, 2, 3)]
    f = fields(material, left, right, density, memb_x, memb_y, bend_table)
    terms, mass, stiff = own_panel(own, f)
    rowwise = Layout(major_to_minor=(0, 1, 2))
    mass, stiff = (with_layout_constraint(v.transpose(1, 0, 2), rowwise) for v in (mass, stiff))
    f, other, terms, mass, stiff = lax.optimization_barrier((f, other, terms, mass, stiff))
    other_core = shifted(other, "c", 1)
    other_core, panels[1:] = lax.optimization_barrier((other_core, panels[1:]))
    olds = (old, old_core, other, other_core)
    parts = panel(1, panels[1], f, olds, terms)
    for d in (3, 2):
        parts = panel(d, panels[d], f, olds, parts)
    parts = jnp.sum(lax.all_to_all(parts, "y", 0, 0), axis=0).reshape(4, 1, PIECE, 4 * M)
    parts = jnp.broadcast_to(parts, (4, 4, PIECE, 4 * M)).reshape(16, PIECE, 4 * M)
    parts = lax.all_to_all(parts, ("x", "zl"), 0, 0).reshape(4, 4, PIECE, 4 * M)
    parts = jnp.sum(parts, axis=1).reshape(1, 4 * PIECE, 4 * M)
    parts = lax.all_to_all(jnp.broadcast_to(parts, (8, 4 * PIECE, 4 * M)), "y", 0, 0)
    area = 1.0 / (R * C * n)
    total = parts.reshape(8, 4, PIECE, 4 * M).transpose(0, 2, 1, 3).reshape(3, M, 16 * M) * area
    return (*[total[i].T for i in range(3)], mass, stiff)


def solution(mesh):
    fine = Mesh(mesh.devices.reshape(8, 4, 4, 2, 2), ("y", "zl", "x", "zh", "c"))
    in_specs = (
        P(MODE, None, SPACE),
        P(MODE, None, SPACE),
        P(None, SPACE),
        P(),
        P(),
        P(),
        P(),
    )
    out_specs = (
        P(None, MODE),
        P(None, MODE),
        P(None, MODE),
        P(MODE, None, SPACE),
        P(MODE, None, SPACE),
    )
    return jax.shard_map(local, mesh=fine, in_specs=in_specs, out_specs=out_specs, check_vma=False)
```

```python
import jax
import jax.numpy as jnp
from jax import lax
from jax.experimental import pallas as pl
from jax.experimental.pallas import tpu as pltpu
from jax.experimental.layout import Layout, with_layout_constraint
from jax.sharding import Mesh, PartitionSpec as P

SPACE = ("y", "zl")
MODE = ("x", "zh", "c")
R, M, C = 64, 32, 128
F32, BF16 = jnp.float32, jnp.bfloat16
VM = pl.BlockSpec(memory_space=pltpu.VMEM)
SM = pl.BlockSpec(memory_space=pltpu.SMEM)


def shifted(value, axis, step):
    n = lax.axis_size(axis)
    return lax.ppermute(value, axis, [(i, (i + step) % n) for i in range(n)])


def select_table(material, values):
    value = jnp.zeros(material.shape, F32)
    for level, entry in enumerate(values):
        value = jnp.where(material == level, entry, value)
    return value


def edges_kernel(u_ref, mat_ref, first_ref, last_ref, sent_ref, mat):
    mat[...] = mat_ref[...].astype(F32)
    sent_ref[0:R] = u_ref[...]
    sent_ref[R : R + 2] = jnp.zeros((2, M, C), BF16)
    pair = lax.broadcasted_iota(jnp.int32, (8, C), 1) // 2
    firsts, lasts = [], []
    for m in range(0, M + 8, 8):
        first = last = jnp.zeros((8, C), F32)
        for r in range(R):
            v = u_ref[r, m : m + 8, :].astype(F32) if m < M else jnp.broadcast_to(mat[r : r + 1, :], (8, C))
            first = jnp.where(pair == r, pltpu.roll(v, 2 * r, 1), first)
            last = jnp.where(pair == r, pltpu.roll(v, (2 * r + 2) % C, 1), last)
        firsts.append(first)
        lasts.append(last)
    first_ref[...] = jnp.concatenate(firsts, axis=0).astype(BF16)
    last_ref[...] = jnp.concatenate(lasts, axis=0).astype(BF16)


def edges(u, material):
    return pl.pallas_call(
        edges_kernel,
        out_shape=[jax.ShapeDtypeStruct((M + 8, C), BF16)] * 2 + [jax.ShapeDtypeStruct((R + 2, M, C), BF16)],
        in_specs=[VM, VM],
        out_specs=[VM] * 3,
        scratch_shapes=[pltpu.VMEM((R, C), F32)],
        cost_estimate=pl.CostEstimate(flops=10**6, bytes_accessed=10**6, transcendentals=0),
    )(u, material)


def fields_kernel(mat_ref, left_ref, right_ref, rho_ref, mx_ref, my_ref, dd_ref, f_ref, kx, ky, rho, dd):
    material = mat_ref[...]
    count = rho_ref.shape[0]
    densities, bends = ([ref[i] for i in range(count)] for ref in (rho_ref, dd_ref))
    mx, my = ([ref[:, i : i + 1].astype(F32) for i in range(count)] for ref in (mx_ref, my_ref))
    kx[...] = jnp.zeros(kx.shape, F32)
    kx[8 : 8 + R, :] = select_table(material, mx)
    ky[...] = select_table(material, my)
    rho[...] = select_table(material, densities)
    dd[...] = select_table(material, bends)
    lane = lax.broadcasted_iota(jnp.int32, (1, C), 1)
    space = lax.axis_index("y") * 4 + lax.axis_index("zl")
    left = select_table(left_ref[M : M + 8, :].astype(F32), my)
    left = jnp.where(space > 0, left, 0.0)
    right = select_table(right_ref[M : M + 8, :].astype(F32), my)
    right = jnp.where(space < 31, right, 0.0)

    for r in range(R):
        k = ky[r : r + 1, :]
        kl = pltpu.roll(left, C - 1 - 2 * r, 1)[0:1]
        kr = pltpu.roll(right, C - 1 - 2 * r, 1)[0:1]
        k8 = jnp.broadcast_to(k, (8, C))
        south = jnp.where(lane == 0, kl, pltpu.roll(k8, 1, 1)[0:1])
        north = jnp.where(lane == C - 1, kr, pltpu.roll(k8, C - 1, 1)[0:1])
        kc = kx[r + 8 : r + 9, :]
        fe = 0.5 * (kc + kx[r + 9 : r + 10, :])
        fw = 0.5 * (kc + kx[r + 7 : r + 8, :])
        fn = 0.5 * (k + north)
        fs = 0.5 * (k + south)
        rr = rho[r : r + 1, :]
        rows = [rr * (2.0 / 3.0), rr * (1.0 / 12.0), fe + fw + fn + fs, fe, fw, fn, fs, dd[r : r + 1, :]]
        f_ref[r] = jnp.concatenate(rows, axis=0)


def fields(material, left, right, density, memb_x, memb_y, bend_table):
    return pl.pallas_call(
        fields_kernel,
        out_shape=jax.ShapeDtypeStruct((R, 8, C), F32),
        in_specs=[VM, VM, VM, SM, VM, VM, SM],
        out_specs=VM,
        scratch_shapes=[pltpu.VMEM((R + 16, C), F32)] + [pltpu.VMEM((R, C), F32)] * 3,
        cost_estimate=pl.CostEstimate(flops=10**6, bytes_accessed=10**6, transcendentals=0),
    )(material, left, right, density, memb_x[None], memb_y[None], bend_table)


PIECE = 3 * M // 8
ROWS = 8


def panel_kernel(d, u_ref, f_ref, *rest):
    if d == 0:
        img, mass_ref, stiff_ref, us, s1, s2, q = rest
    else:
        olds, own_ref = rest[:4], rest[4]
        out_ref, us, s1, s2, q, img, acc = rest[5:]
    zero = jnp.zeros((M, C), F32)
    for r in (0, 1, R + 2, R + 3):
        us[r] = zero
    s1[0] = zero
    s1[R + 1] = zero
    lane = lax.broadcasted_iota(jnp.int32, (1, C), 1)
    left = u_ref[R].astype(F32)
    right = u_ref[R + 1].astype(F32)
    first = jnp.where(lane % 2 == 0, right, left)
    right = pltpu.roll(right, C - 2, 1)
    second = [jnp.where((lane // 2) % 2 == p, left, right) for p in (0, 1)]

    for r in range(R):
        u = u_ref[r].astype(F32)
        h1 = pltpu.roll(first, C - 1 - 2 * r, 1)
        h2 = pltpu.roll(second[r % 2], (C - 2 * r) % C, 1)
        south = jnp.where(lane == 0, h1, pltpu.roll(u, 1, 1))
        south2 = jnp.where(lane < 2, h2, pltpu.roll(u, 2, 1))
        north = jnp.where(lane == C - 1, h1, pltpu.roll(u, C - 1, 1))
        north2 = jnp.where(lane >= C - 2, h2, pltpu.roll(u, C - 2, 1))
        us[r + 2] = u
        s1[r + 1] = south + north
        s2[r] = south2 + north2
        q[r] = f_ref[r, 5:6, :] * north + f_ref[r, 6:7, :] * south

    if d > 0:
        acc[...] = jnp.zeros(acc.shape, F32)

    def rows(step, slot):
        base = step * ROWS
        for j in range(ROWS):
            r = base + j
            u, east, west = us[r + 2], us[r + 3], us[r + 1]
            near = (east + west) + s1[r + 1]
            mass = f_ref[r, 0:1, :] * u + f_ref[r, 1:2, :] * near
            membrane = f_ref[r, 2:3, :] * u - f_ref[r, 3:4, :] * east - f_ref[r, 4:5, :] * west - q[r]
            far = (us[r + 4] + us[r]) + s2[r]
            diagonal = s1[r] + s1[r + 2]
            bending = f_ref[r, 7:8, :] * (20.0 * u - 8.0 * near + 2.0 * diagonal + far)
            for i, v in enumerate((mass, membrane, bending)):
                hi = v.astype(BF16)
                lo = (v - hi.astype(F32)).astype(BF16)
                img[slot, M * i : M * i + M, C * j : C * j + C] = hi
                img[slot, M * (i + 3) : M * (i + 3) + M, C * j : C * j + C] = lo
            if d == 0:
                mass_ref[r] = mass.astype(BF16)
                stiff_ref[r] = (membrane + bending).astype(BF16)
        if d == 0:
            return
        wide = [jnp.concatenate([o[base + j] for j in range(ROWS)], axis=1) for o in olds]
        wide = jnp.concatenate(wide, axis=0)
        dims = (((1,), (1,)), ((), ()))
        acc[0] += lax.dot_general(img[slot], wide, dims, preferred_element_type=F32)
        if d == 1:
            acc[1] += lax.dot_general(own_ref[step], wide, dims, preferred_element_type=F32)

    for step in range(R // ROWS):
        rows(step, step if d == 0 else step % 2)
    if d == 0:
        return
    zh, c = lax.axis_index("zh"), lax.axis_index("c")
    lane = lax.broadcasted_iota(jnp.int32, (1, 4 * M), 1)
    for i, away in enumerate((d, 0) if d == 1 else (d,)):
        v = pltpu.roll(acc[i, 0 : 3 * M] + acc[i, 3 * M : 6 * M], zh * 64, 1)
        swapped = jnp.where(lane % 64 < 32, pltpu.roll(v, 96, 1), pltpu.roll(v, 32, 1))
        v = jnp.where(c == 1, swapped, v)
        put(out_ref, v, lax.rem(lax.axis_index("x") + away, 4))


def put(out_ref, v, chip):
    for k in range(4):

        @pl.when(chip == k)
        def _():
            for i in range(8):
                out_ref[i, PIECE * k : PIECE * k + PIECE] = v[PIECE * i : PIECE * i + PIECE]


TERMS = (R // ROWS, 6 * M, ROWS * C)


def fields_scratch():
    shapes = ((R + 4, M, C), (R + 2, M, C), (R, M, C), (R, M, C))
    return [pltpu.VMEM(shape, F32) for shape in shapes]


def own_panel(u, f):
    return pl.pallas_call(
        lambda *refs: panel_kernel(0, *refs),
        out_shape=[jax.ShapeDtypeStruct(TERMS, BF16)] + [jax.ShapeDtypeStruct((R, M, C), BF16)] * 2,
        in_specs=[VM] * 2,
        out_specs=[VM] * 3,
        scratch_shapes=fields_scratch(),
        compiler_params=pltpu.CompilerParams(vmem_limit_bytes=20 * 2**20),
        cost_estimate=pl.CostEstimate(flops=4 * 10**8, bytes_accessed=4 * 10**6, transcendentals=0),
    )(u, f)


def panel(d, u, f, olds, extra):
    operands = [u, f, *olds, extra]
    return pl.pallas_call(
        lambda *refs: panel_kernel(d, *refs),
        out_shape=jax.ShapeDtypeStruct((8, 4 * PIECE, 4 * M), F32),
        in_specs=[VM] * 6 + [VM if d == 1 else pl.BlockSpec(memory_space=pl.ANY)],
        out_specs=VM,
        input_output_aliases={} if d == 1 else {6: 0},
        scratch_shapes=fields_scratch()
        + [pltpu.VMEM((2, 6 * M, ROWS * C), BF16), pltpu.VMEM((2 if d == 1 else 1, 6 * M, 4 * M), F32)],
        compiler_params=pltpu.CompilerParams(vmem_limit_bytes=20 * 2**20),
        cost_estimate=pl.CostEstimate(flops=4 * 10**8, bytes_accessed=4 * 10**6, transcendentals=0),
    )(*operands)


def local(old_modes, new_modes, material, density, memb_x, memb_y, bend_table):
    first, last, sent = edges(new_modes.transpose(1, 0, 2), material)
    first, last, old_modes = lax.optimization_barrier((first, last, old_modes))
    old = old_modes.transpose(1, 0, 2)
    other = shifted(old, "zh", 1)
    old_core = shifted(old, "c", 1)
    n = 32
    left = lax.ppermute(last, SPACE, [(i, i + 1) for i in range(n - 1)])
    right = lax.ppermute(first, SPACE, [(i + 1, i) for i in range(n - 1)])
    own = lax.dynamic_update_slice(sent, jnp.stack([left[:M], right[:M]]), (R, 0, 0))
    panels = [own] + [shifted(own, "x", -d) for d in (1, 2, 3)]
    f = fields(material, left, right, density, memb_x, memb_y, bend_table)
    terms, mass, stiff = own_panel(own, f)
    rowwise = Layout(major_to_minor=(0, 1, 2))
    mass, stiff = (with_layout_constraint(v.transpose(1, 0, 2), rowwise) for v in (mass, stiff))
    f, other, terms, mass, stiff = lax.optimization_barrier((f, other, terms, mass, stiff))
    other_core = shifted(other, "c", 1)
    other_core, panels[1], panels[3] = lax.optimization_barrier((other_core, panels[1], panels[3]))
    olds = (old, old_core, other, other_core)
    parts = panel(1, panels[1], f, olds, terms)
    for d in (3, 2):
        parts = panel(d, panels[d], f, olds, parts)
    parts = jnp.sum(lax.all_to_all(parts, "y", 0, 0), axis=0).reshape(4, 1, PIECE, 4 * M)
    parts = jnp.broadcast_to(parts, (4, 4, PIECE, 4 * M)).reshape(16, PIECE, 4 * M)
    parts = lax.all_to_all(parts, ("x", "zl"), 0, 0).reshape(4, 4, PIECE, 4 * M)
    parts = jnp.sum(parts, axis=1).reshape(1, 4 * PIECE, 4 * M)
    parts = lax.all_to_all(jnp.broadcast_to(parts, (8, 4 * PIECE, 4 * M)), "y", 0, 0)
    area = 1.0 / (R * C * n)
    total = parts.reshape(8, 4, PIECE, 4 * M).transpose(0, 2, 1, 3).reshape(3, M, 16 * M) * area
    return (*[total[i].T for i in range(3)], mass, stiff)


def solution(mesh):
    fine = Mesh(mesh.devices.reshape(8, 4, 4, 2, 2), ("y", "zl", "x", "zh", "c"))
    in_specs = (
        P(MODE, None, SPACE),
        P(MODE, None, SPACE),
        P(None, SPACE),
        P(),
        P(),
        P(),
        P(),
    )
    out_specs = (
        P(None, MODE),
        P(None, MODE),
        P(None, MODE),
        P(MODE, None, SPACE),
        P(MODE, None, SPACE),
    )
    return jax.shard_map(local, mesh=fine, in_specs=in_specs, out_specs=out_specs, check_vma=False)
```
